128 devices in a mesh: dp: 128 (over x, y, z, core).
Axes of the slice: x: 4, y: 4, z: 4, core: 2. Of those that a mesh axis runs over, the one named last changes fastest.
Arguments:
- tokens: bfloat16 [256, 512, 576], P('dp'), may hold values from -6 to 6
- positions: int32 [256, 512], P('dp'), may hold values from 0 to 8191, as said below
- norm_gains: bfloat16 [1152], P('dp'), may hold values from 0.25 to 1.75
- w_query: bfloat16 [331776], P('dp'), may hold values from -0.25 to 0.25
- w_key: bfloat16 [110592], P('dp'), may hold values from -0.25 to 0.25
- w_value: bfloat16 [110592], P('dp'), may hold values from -0.25 to 0.25
- w_out: bfloat16 [331776], P('dp'), may hold values from -1 to 1
- w_gate: bfloat16 [884736], P('dp'), may hold values from -0.25 to 0.25
- w_up: bfloat16 [884736], P('dp'), may hold values from -0.25 to 0.25
- w_down: bfloat16 [884736], P('dp'), may hold values from -0.3125 to 0.3125
- cotangent: float32 [256, 512, 576], P('dp')
Outputs:
- output: bfloat16 [256, 512, 576], P('dp')
- grad_tokens: float32 [256, 512, 576], P('dp')
- grad_gains: float32 [1152], P('dp')
- grad_query: float32 [331776], P('dp')
- grad_key: float32 [110592], P('dp')
- grad_value: float32 [110592], P('dp')
- grad_out: float32 [331776], P('dp')
- grad_gate: float32 [884736], P('dp')
- grad_up: float32 [884736], P('dp')
- grad_down: float32 [884736], P('dp')
The draws below stay inside these ranges and needn't reach their ends.
Inputs may be any that keep to these rules, and one draw needn't show every extreme that they name: Each row is a run of packed documents: positions count up by one within a document, and every document after a row's first starts at 0; in every draw one row starts at 0, and one row is a single document that ends at 8191.
All inputs are finite; a program needn't handle non-finite values.
Results may differ from the reference program's by a relative error of at most 0.015.
Values may be sent and summed in bfloat16 or wider, within the bound.
No kernel may reach another device: no remote copies, remote signals or barrier semaphores. Data moves between devices by JAX's collectives and lax.ppermute only.
A program may use at most 192 MiB of HBM per device.

```python
import math
import jax
import jax.numpy as jnp
from jax import lax

D = 576
HEADS = 9
KV_HEADS = 3
HEAD = 64
FF = 1536
CONTEXT = 8192
SEQ_LEN = 512
SEQS = 256


def draw_positions(key, part):
    key = jax.random.fold_in(key, 3)
    key_start, key_break, key_pick = jax.random.split(key, 3)
    offsets = jax.random.randint(key_start, (SEQS,), 0, CONTEXT - SEQ_LEN + 1)
    lowest = jax.random.randint(key_pick, (), 0, SEQS)
    highest = (lowest + SEQS // 2) % SEQS
    offsets = offsets.at[lowest].set(0).at[highest].set(CONTEXT - SEQ_LEN)
    index = jnp.arange(SEQ_LEN, dtype=jnp.int32)
    breaks = jax.random.randint(key_break, (SEQS, SEQ_LEN), 0, max(2, SEQ_LEN // 4)) == 0
    breaks = breaks & (index[None, :] > 0)
    breaks = breaks & (jnp.arange(SEQS, dtype=jnp.int32)[:, None] != highest)
    starts = lax.cummax(jnp.where(breaks, index[None, :], 0), axis=1)
    shifted = jnp.where(starts == 0, offsets[:, None], 0)
    return (index[None, :] - starts + shifted).astype(jnp.int32)


def draw_cotangent(key, part):
    key = jax.random.fold_in(key, 11)
    ramp_up = jnp.arange(SEQS, dtype=jnp.float32) / (SEQS - 1)
    values = jax.random.normal(key, (SEQS, SEQ_LEN, D), jnp.float32)
    rising = jnp.exp(jnp.log(3.0) * ramp_up)
    return values * rising[:, None, None] / 1.7


def block_scale(own_key, dims, cuts, smallest, largest):
    factor_of, own = 1.0, jax.random.fold_in(own_key, 6)
    for dim, blocks in cuts:
        draws = jnp.exp(jax.random.uniform(jax.random.fold_in(own, dim), (blocks,), jnp.float32, smallest / len(cuts), largest / len(cuts)))
        factor_of = factor_of * jnp.repeat(draws, dims[dim] // blocks).reshape([-1 if axis == dim else 1 for axis in range(len(dims))])
    return factor_of


def gaussian(own_key, dims, deviation, limit, cuts=(), kind=jnp.bfloat16):
    values = deviation * jax.random.normal(own_key, dims, jnp.float32)
    if cuts:
        values = values * block_scale(own_key, dims, cuts, -0.22, 0.18)
    return jnp.clip(values, -limit, limit).astype(kind)


def setup_inputs(seed: int = 0) -> dict:
    arg_keys = jax.random.split(jax.random.key(seed), 12)
    tokens = gaussian(arg_keys[0], (SEQS, SEQ_LEN, D), 1.0, 6.0, ((0, 128),))
    positions = draw_positions(jax.random.fold_in(arg_keys[11], 71), 0)
    norm_gains = jnp.clip(1.0 + 0.15 * jax.random.normal(arg_keys[2], (2 * D,), jnp.float32), 0.25, 1.75).astype(jnp.bfloat16)
    w_query = gaussian(arg_keys[3], (D * D,), D ** -0.5, 0.25, ((0, 128),))
    w_key = gaussian(arg_keys[4], (D * KV_HEADS * HEAD,), D ** -0.5, 0.25, ((0, 128),))
    w_value = gaussian(arg_keys[5], (D * KV_HEADS * HEAD,), D ** -0.5, 0.25, ((0, 128),))
    w_out = gaussian(arg_keys[6], (D * D,), (D // 16) ** -0.5, 1.0, ((0, 128),))
    w_gate = gaussian(arg_keys[7], (D * FF,), D ** -0.5, 0.25, ((0, 128),))
    w_up = gaussian(arg_keys[8], (D * FF,), D ** -0.5, 0.25, ((0, 128),))
    w_down = gaussian(arg_keys[9], (FF * D,), (FF // 4) ** -0.5, 0.3125, ((0, 128),))
    cotangent = draw_cotangent(jax.random.fold_in(arg_keys[11], 71), 0)
    return dict(tokens=tokens, positions=positions, norm_gains=norm_gains, w_query=w_query, w_key=w_key, w_value=w_value, w_out=w_out, w_gate=w_gate, w_up=w_up, w_down=w_down, cotangent=cotangent)


EPSILON = 1e-05
HIGHEST = lax.Precision.HIGHEST

@jax.custom_vjp
def low(v):
    return lax.optimization_barrier(v.astype(jnp.bfloat16)).astype(jnp.float32)

@jax.custom_vjp
def low_back(v):
    return v

def low_keep(v):
    return (low(v), None)

def low_pass(kept, grad):
    return (grad,)

def back_keep(v):
    return (v, None)

def back_low(kept, grad):
    return (low(grad),)
low.defvjp(low_keep, low_pass)
low_back.defvjp(back_keep, back_low)

def rms_scale(values):
    return values * lax.rsqrt(lax.optimization_barrier(jnp.mean(values * values, axis=-1, keepdims=True)) + EPSILON)

def rot_tables(places):
    freqs = 100000.0 ** (-(jnp.arange(HEAD // 2, dtype=jnp.float32) * 2.0 / HEAD))
    angles = places.astype(jnp.float32)[..., None] * freqs
    angles = jnp.concatenate([angles, angles], axis=-1)
    return (jnp.cos(angles)[:, :, None, :], jnp.sin(angles)[:, :, None, :])

def rotate(values, cos_table, sin_table):
    half_dim = values.shape[-1] // 2
    turned = jnp.concatenate([-values[..., half_dim:], values[..., :half_dim]], axis=-1)
    return values * cos_table + turned * sin_table

def project(values, matrix):
    return jnp.einsum('bsc,cd->bsd', values, matrix, precision=HIGHEST)

def document_mask(places):
    places = places.astype(jnp.int32)
    fresh = (places[:, 1:] != places[:, :-1] + 1).astype(jnp.int32)
    openers = jnp.concatenate([jnp.zeros((places.shape[0], 1), jnp.int32), fresh], axis=1)
    doc_ids = jnp.cumsum(openers, axis=1)
    index = jnp.arange(places.shape[1], dtype=jnp.int32)
    same_doc = doc_ids[:, None, :] == doc_ids[:, :, None]
    earlier = index[None, :] <= index[:, None]
    return same_doc & earlier[None]

def layer(inputs, places, gain_vec, query_flat, key_flat, value_flat, out_flat, gate_flat, up_flat, down_flat):
    batch_size = inputs.shape[0]
    per_group = HEADS // KV_HEADS
    kv_width = KV_HEADS * HEAD
    gain_one = gain_vec[:D]
    gain_two = gain_vec[D:]
    m_query = query_flat.reshape(D, D)
    m_key = key_flat.reshape(D, kv_width)
    m_value = value_flat.reshape(D, kv_width)
    m_out = out_flat.reshape(D, D)
    m_gate = gate_flat.reshape(D, FF)
    m_up = up_flat.reshape(D, FF)
    m_down = down_flat.reshape(FF, D)
    cos_table, sin_table = rot_tables(places)
    h_one = low(rms_scale(inputs) * gain_one)
    q_raw = low_back(project(h_one, m_query)).reshape(batch_size, SEQ_LEN, HEADS, HEAD)
    q_rot = low(rotate(q_raw, cos_table, sin_table)).reshape(batch_size, SEQ_LEN, KV_HEADS, per_group, HEAD)
    k_raw = low_back(project(h_one, m_key)).reshape(batch_size, SEQ_LEN, KV_HEADS, HEAD)
    k_rot = low(rotate(k_raw, cos_table, sin_table))
    v_vals = low(low_back(project(h_one, m_value))).reshape(batch_size, SEQ_LEN, KV_HEADS, HEAD)
    scores = low_back(jnp.einsum('bsgjd,btgd->bgjst', q_rot, k_rot, precision=HIGHEST) * 0.125)
    allowed = document_mask(places)
    scores = jnp.where(allowed[:, None, None], scores, -1e+30)
    attn_probs = low(jax.nn.softmax(scores, axis=-1))
    mixed_heads = jnp.einsum('bgjst,btgd->bsgjd', attn_probs, v_vals, precision=HIGHEST)
    heads_out = low(low_back(mixed_heads)).reshape(batch_size, SEQ_LEN, D)
    x_mid = inputs + low_back(project(heads_out, m_out))
    h_two = low(rms_scale(x_mid) * gain_two)
    gate_in = low_back(project(h_two, m_gate))
    up_in = low_back(project(h_two, m_up))
    mixed_act = low(jax.nn.silu(gate_in) * up_in)
    return x_mid + low_back(project(mixed_act, m_down))

def reference(tokens, positions, norm_gains, w_query, w_key, w_value, w_out, w_gate, w_up, w_down, cotangent):
    params = tuple((p.astype(jnp.float32) for p in (norm_gains, w_query, w_key, w_value, w_out, w_gate, w_up, w_down)))
    per_step = math.gcd(SEQS, max(1, 4096 // SEQ_LEN))
    steps_all = SEQS // per_step
    stacked = (tokens.reshape(steps_all, per_step, SEQ_LEN, D), positions.reshape(steps_all, per_step, SEQ_LEN).astype(jnp.int32), cotangent.reshape(steps_all, per_step, SEQ_LEN, D))

    def one_step(totals, item):
        inputs, places, upstream = item

        def apply_layer(x_in, *weights):
            return layer(x_in, places, *weights)
        result, pullback = jax.vjp(apply_layer, inputs.astype(jnp.float32), *params)
        grads = pullback(upstream.astype(jnp.float32))
        totals = tuple((total + grad for total, grad in zip(totals, grads[1:])))
        return (totals, (result.astype(jnp.bfloat16), grads[0]))
    start_totals = tuple((jnp.zeros(p.shape, jnp.float32) for p in params))
    final, (results, in_grads) = lax.scan(jax.checkpoint(one_step), start_totals, stacked)
    return (results.reshape(SEQS, SEQ_LEN, D), in_grads.reshape(SEQS, SEQ_LEN, D), final[0], final[1], final[2], final[3], final[4], final[5], final[6], final[7])
```

```python
import jax
import jax.numpy as jnp
from jax import lax
from jax.sharding import PartitionSpec as P
from jax.experimental import pallas as pl
from jax.experimental.pallas import tpu as pltpu

D = 576
HEADS = 9
KV_HEADS = 3
HEAD = 64
FF = 1536
SEQ = 512
KVW = KV_HEADS * HEAD
QKV = D + 2 * KVW
HALF = SEQ // 2

EPSILON = 1e-05
NEG_FILL = -1e30

F32 = jnp.float32
BF16 = jnp.bfloat16

CHIPS = 64
R_GATE = 54
R_DOWN = 60
R_OUT = 27
R_KEY = 9
A_QUERY, A_KEY, A_VALUE, A_GAIN, A_DOWN, A_OUT, ROWS_A = 0, 27, 36, 45, 48, 108, 144
B_GATE, B_UP, ROWS_B = 0, 54, 112
G_DOWN, G_OUT, ROWS_G = 0, 60, 96
Q_QUERY, Q_KEY, Q_VALUE, Q_GAIN, ROWS_Q = 0, 27, 36, 45, 48

NN = (((1,), (0,)), ((), ()))
NT = (((1,), (1,)), ((), ()))
TN = (((0,), (0,)), ((), ()))


def mm(a, b, dims=NN):
    return lax.dot_general(a, b, dims, preferred_element_type=F32)


def whole_spec(shape):
    zeros = (0,) * len(shape)
    return pl.BlockSpec(shape, lambda i: zeros)


def seq_spec(shape, at=None):
    zeros = (0,) * len(shape)
    return pl.BlockSpec((1,) + shape, lambda i: (i if at is None else at,) + zeros)


def chip_of(slot, where_ref, swap, sign):
    one, two, three = slot // 16, (slot // 4) % 4, slot % 4
    kz, ky = (two, one) if swap else (one, two)
    x = (where_ref[1] + sign * three + 4) % 4
    y = (where_ref[2] + sign * ky + 4) % 4
    z = (where_ref[3] + sign * kz + 4) % 4
    return (x * 4 + y) * 4 + z


def put_rows(ref, dev, rows, val):
    ref[pl.ds(dev * rows, rows), :] = val


def get_rows(ref, dev, rows):
    return ref[pl.ds(dev * rows, rows), :]


def split_square(ref):
    parts = []
    for half in range(2):
        for j in range(3):
            piece = ref[pl.ds(3 * half + j, D, stride=6), :]
            parts.append(piece if j < 2 else piece[:, :32])
    return parts


def join_square(ref, val_ref):
    for half in range(2):
        for j in range(3):
            width = 128 if j < 2 else 32
            at = 288 * half + 128 * j
            ref[pl.ds(3 * half + j, D, stride=6), :width] = val_ref[:, at : at + width]


def pack_kernel(wqo, wkv, gn, wd, wgu, out_ref, stage_ref):
    stage_ref[...] = jnp.zeros_like(stage_ref)
    square = wqo[...].astype(F32)
    thin = wkv[...].astype(F32)
    for at, val in (
        (A_QUERY, square[:R_OUT]),
        (A_OUT, square[R_OUT:]),
        (A_KEY, thin[:R_KEY]),
        (A_VALUE, thin[R_KEY:]),
        (A_GAIN, gn[...].astype(F32)),
        (A_DOWN, wd[...].astype(F32)),
        (ROWS_A, wgu[...].astype(F32)),
    ):
        stage_ref[at : at + val.shape[0], : val.shape[1]] = val
    out_ref[...] = stage_ref[...].astype(BF16)


def pack(pieces):
    vmem = pl.BlockSpec(memory_space=pltpu.VMEM)
    return pl.pallas_call(
        pack_kernel,
        in_specs=[vmem] * 5,
        out_specs=vmem,
        out_shape=jax.ShapeDtypeStruct((ROWS_A + ROWS_B, 128), BF16),
        scratch_shapes=[pltpu.VMEM((ROWS_A + ROWS_B, 128), F32)],
        name="pack",
    )(*pieces)


def lane_rows(v, rows, width):
    v = v.reshape(rows, width)
    full = -(-width // 128) * 128
    v = jnp.pad(v, ((0, 0), (0, full - width)))
    return v.reshape(rows * full // 128, 128)


def take_lanes(v, rows, width):
    full = -(-width // 128) * 128
    return v.reshape(rows, full)[:, :width].reshape(-1)


def rope_rows(v, cos_t, sin_t, heads, sign):
    out = []
    for head in range(heads):
        lo = v[head * HEAD : head * HEAD + 32]
        hi = v[head * HEAD + 32 : head * HEAD + 64]
        if sign > 0:
            out += [lo * cos_t - hi * sin_t, hi * cos_t + lo * sin_t]
        else:
            out += [lo * cos_t + hi * sin_t, hi * cos_t - lo * sin_t]
    return jnp.concatenate(out, axis=0)


def attn_fwd_kernel(
    where_ref, own_ref, other_ref, x_ref, cos_ref, sin_ref, docr_ref, docc_ref,
    wqkv_ref, gain_ref, h_t_ref, q_t_ref, k_t_ref, v_t_ref, p_ref, o_t_ref,
    qs_ref, ks_ref, vs_ref, gs_ref, w_t_ref, bias_ref, k_ref,
):
    @pl.when(pl.program_id(0) == 0)
    def _():
        core = where_ref[0]

        def squeeze(slot, carry):
            chip = chip_of(slot, where_ref, False, -1)
            for ref, side in ((own_ref, core), (other_ref, 1 - core)):
                dev = chip * 2 + side
                val = ref[slot, 0:48, :].astype(F32)
                put_rows(qs_ref, dev, R_OUT, val[A_QUERY : A_QUERY + R_OUT])
                put_rows(ks_ref, dev, R_KEY, val[A_KEY : A_KEY + R_KEY])
                put_rows(vs_ref, dev, R_KEY, val[A_VALUE : A_VALUE + R_KEY])
                put_rows(gs_ref, dev, 1, val[A_GAIN : A_GAIN + 1])
            return carry

        lax.fori_loop(0, CHIPS, squeeze, 0)
        parts = split_square(qs_ref)
        for ref in (ks_ref, vs_ref):
            for half in range(2):
                parts.append(ref[pl.ds(half, D, stride=2), :][:, :96])
        whole = jnp.concatenate(parts, axis=1)
        wqkv_ref[...] = whole.astype(BF16)
        w_t_ref[...] = whole.T.astype(BF16)
        for lane in range(9):
            gain_ref[pl.ds(lane, 2 * CHIPS, stride=9), :] = gs_ref[:, lane : lane + 1]

    x = x_ref[0].astype(F32)
    inv = lax.rsqrt(jnp.mean(x * x, axis=0, keepdims=True) + EPSILON)
    h_t = ((x * inv) * gain_ref[:D]).astype(BF16)
    h_t_ref[0] = h_t
    cos_t = cos_ref[0]
    sin_t = sin_ref[0]
    q_t = mm(w_t_ref[:D], h_t)
    q_t_ref[0] = rope_rows(q_t, cos_t, sin_t, HEADS, 1).astype(BF16) * 0.125
    k_t = rope_rows(mm(w_t_ref[D : D + KVW], h_t), cos_t, sin_t, KV_HEADS, 1).astype(BF16)
    k_t_ref[0] = k_t
    for group in range(KV_HEADS):
        k_ref[group] = k_t[group * HEAD : (group + 1) * HEAD].astype(F32).T.astype(BF16)
    v_t_ref[0] = mm(w_t_ref[D + KVW :], h_t).astype(BF16)
    key_at = lax.broadcasted_iota(jnp.int32, (SEQ, SEQ), 0)
    query_at = lax.broadcasted_iota(jnp.int32, (SEQ, SEQ), 1)
    same = docc_ref[0] == docr_ref[0]
    bias_ref[...] = jnp.where(same & (key_at <= query_at), 0.0, NEG_FILL)

    def group_step(group, carry):
        kv_rows = pl.ds(pl.multiple_of(group * HEAD, HEAD), HEAD)
        for member in range(HEADS // KV_HEADS):
            head = group * (HEADS // KV_HEADS) + member
            rows = pl.ds(pl.multiple_of(head * HEAD, HEAD), HEAD)
            for block in range(2):
                cols = slice(block * HALF, (block + 1) * HALF)
                keys = slice(0, (block + 1) * HALF)
                s_t = mm(k_ref[group, keys, :], q_t_ref[0, rows, cols]) + bias_ref[keys, cols]
                peak = jnp.max(s_t, axis=0, keepdims=True)
                e_t = jnp.exp(s_t - peak)
                scale = 1.0 / jnp.sum(e_t, axis=0, keepdims=True)
                p_t = (e_t * scale).astype(BF16)
                p_ref[0, head, keys, cols] = p_t
                o_t_ref[0, rows, cols] = mm(v_t_ref[0, kv_rows, keys], p_t).astype(BF16)
        return carry

    lax.fori_loop(0, KV_HEADS, group_step, 0)


def attn_fwd(where, own, other, x_t, cos_t, sin_t, doc_row, doc_col):
    seqs = x_t.shape[0]
    out = [
        ((D, QKV), BF16, False),
        ((2 * D, 1), F32, False),
        ((D, SEQ), BF16, True),
        ((D, SEQ), BF16, True),
        ((KVW, SEQ), BF16, True),
        ((KVW, SEQ), BF16, True),
        ((HEADS, SEQ, SEQ), BF16, True),
        ((D, SEQ), BF16, True),
    ]
    return pl.pallas_call(
        attn_fwd_kernel,
        grid=(seqs,),
        in_specs=[
            pl.BlockSpec(memory_space=pltpu.SMEM),
            whole_spec((CHIPS, ROWS_A, 128)),
            whole_spec((CHIPS, ROWS_A, 128)),
            seq_spec((D, SEQ)),
            seq_spec((32, SEQ)),
            seq_spec((32, SEQ)),
            seq_spec((1, SEQ)),
            seq_spec((SEQ, 1)),
        ],
        out_specs=[seq_spec(s) if per else whole_spec(s) for s, _, per in out],
        out_shape=[jax.ShapeDtypeStruct(((seqs,) + s) if per else s, t) for s, t, per in out],
        scratch_shapes=[
            pltpu.VMEM((2 * CHIPS * R_OUT, 128), F32),
            pltpu.VMEM((2 * CHIPS * R_KEY, 128), F32),
            pltpu.VMEM((2 * CHIPS * R_KEY, 128), F32),
            pltpu.VMEM((2 * CHIPS, 128), F32),
            pltpu.VMEM((QKV, D), BF16),
            pltpu.VMEM((SEQ, SEQ), F32),
            pltpu.VMEM((KV_HEADS, SEQ, HEAD), BF16),
        ],
        compiler_params=pltpu.CompilerParams(vmem_limit_bytes=34 * 2**20),
        cost_estimate=pl.CostEstimate(
            flops=8 * 10**9, bytes_accessed=20 * 10**6, transcendentals=5 * 10**6
        ),
        name="attn_fwd",
    )(where, own, other, x_t, cos_t, sin_t, doc_row, doc_col)


CHUNK = 256
CHUNKS = FF // CHUNK


def ffn_kernel(
    where_ref, a_own_ref, a_other_ref, b_own_ref, b_other_ref, x_ref, o_t_ref, cot_ref, gain_ref,
    y_ref, dx1_ref, do_t_ref, dgain_ref, send_g_ref, keep_g_ref, send_b_ref, keep_b_ref,
    gs_ref, us_ref, ds_ref, os_ref, wg_ref, wu_ref, wd_ref, wo_ref,
    acc_ref, h_t_ref, gb_ref, dh_ref, inv_ref, stage_ref,
):
    seqs = x_ref.shape[0]
    core = where_ref[0]

    def squeeze(slot, carry):
        chip = chip_of(slot, where_ref, False, -1)
        for ref, side in ((a_own_ref, core), (a_other_ref, 1 - core)):
            dev = chip * 2 + side
            val = ref[slot, 48:ROWS_A, :].astype(F32)
            put_rows(ds_ref, dev, R_DOWN, val[A_DOWN - 48 : A_DOWN - 48 + R_DOWN])
            put_rows(os_ref, dev, R_OUT, val[A_OUT - 48 : A_OUT - 48 + R_OUT])
        chip = chip_of(slot, where_ref, True, -1)
        for ref, side in ((b_own_ref, core), (b_other_ref, 1 - core)):
            dev = chip * 2 + side
            val = ref[slot].astype(F32)
            put_rows(gs_ref, dev, R_GATE, val[B_GATE : B_GATE + R_GATE])
            put_rows(us_ref, dev, R_GATE, val[B_UP : B_UP + R_GATE])
        return carry

    lax.fori_loop(0, CHIPS, squeeze, 0)
    wo_ref[...] = jnp.concatenate(split_square(os_ref), axis=1).astype(BF16)
    for j in range(12):
        cols = slice(j * 128, (j + 1) * 128)
        wg_ref[:, cols] = gs_ref[pl.ds(j, D, stride=12), :].astype(BF16)
        wu_ref[:, cols] = us_ref[pl.ds(j, D, stride=12), :].astype(BF16)
    for j in range(5):
        width = min(128, D - j * 128)
        wd_ref[:, j * 128 : j * 128 + width] = ds_ref[pl.ds(j, FF, stride=5), :][:, :width].astype(BF16)

    gain = gain_ref[D:]
    for seq in range(seqs):
        cols = slice(seq * SEQ, (seq + 1) * SEQ)
        x1 = x_ref[seq].astype(F32) + mm(wo_ref[...], o_t_ref[seq], TN)
        inv = lax.rsqrt(jnp.mean(x1 * x1, axis=0, keepdims=True) + EPSILON)
        normed = x1 * inv
        acc_ref[:, cols] = x1
        inv_ref[:, cols] = inv
        dx1_ref[seq] = normed
        h_t_ref[:, cols] = (normed * gain).astype(BF16)
        gb_ref[:, cols] = cot_ref[seq].astype(BF16)
    dh_ref[...] = jnp.zeros_like(dh_ref)

    def chunk_step(chunk, carry):
        cols = pl.ds(pl.multiple_of(chunk * CHUNK, CHUNK), CHUNK)
        wg = wg_ref[:, cols]
        wu = wu_ref[:, cols]
        wd = wd_ref[cols, :]
        h_t = h_t_ref[...]
        gb = gb_ref[...]
        a = mm(wg, h_t, TN)
        b = mm(wu, h_t, TN)
        dm = mm(wd, gb)
        sg = 1.0 / (1.0 + jnp.exp(-a))
        silu = a * sg
        m = (silu * b).astype(BF16)
        da = (dm * b * sg * (1.0 + a * (1.0 - sg))).astype(BF16)
        db = (dm * silu).astype(BF16)
        acc_ref[...] += mm(wd, m, TN)
        dh_ref[...] += mm(wg, da) + mm(wu, db)
        dwg = mm(h_t, da, NT)
        dwu = mm(h_t, db, NT)
        dwd = mm(m, gb, NT)
        for j in range(CHUNK // 128):
            lane = slice(j * 128, (j + 1) * 128)
            at = chunk * (CHUNK // 128) + j
            gs_ref[pl.ds(at, D, stride=12), :] = dwg[:, lane]
            us_ref[pl.ds(at, D, stride=12), :] = dwu[:, lane]
        for j in range(5):
            width = min(128, D - j * 128)
            ds_ref[pl.ds(chunk * CHUNK * 5 + j, CHUNK, stride=5), :width] = dwd[
                :, j * 128 : j * 128 + width
            ]
        return carry

    lax.fori_loop(0, CHUNKS, chunk_step, 0)

    dgain = jnp.zeros((D, 1), F32)
    dwo = jnp.zeros((D, D), F32)
    for seq in range(seqs):
        cols = slice(seq * SEQ, (seq + 1) * SEQ)
        y_ref[seq] = acc_ref[:, cols].astype(BF16)
        dh = dh_ref[:, cols]
        normed = dx1_ref[seq]
        dgain += jnp.sum(dh * normed, axis=1, keepdims=True)
        dn = dh * gain
        dx1 = cot_ref[seq] + inv_ref[:, cols] * (
            dn - normed * jnp.mean(dn * normed, axis=0, keepdims=True)
        )
        dx1_ref[seq] = dx1
        low = dx1.astype(BF16)
        dwo += mm(o_t_ref[seq], low, NT)
        do_t_ref[seq] = mm(wo_ref[...], low).astype(BF16)
    dgain_ref[...] = dgain
    dh_ref[:, :D] = dwo
    join_square(os_ref, dh_ref)

    stage_ref[...] = jnp.zeros_like(stage_ref)

    def spread(slot, carry):
        for keep_it in range(2):
            chip = chip_of(slot, where_ref, False, 1)
            dev = chip * 2 + (core if keep_it else 1 - core)
            stage_ref[G_DOWN : G_DOWN + R_DOWN, :] = get_rows(ds_ref, dev, R_DOWN)
            stage_ref[G_OUT : G_OUT + R_OUT, :] = get_rows(os_ref, dev, R_OUT)
            (keep_g_ref if keep_it else send_g_ref)[slot] = stage_ref[:ROWS_G].astype(BF16)
            chip = chip_of(slot, where_ref, True, 1)
            dev = chip * 2 + (core if keep_it else 1 - core)
            stage_ref[B_GATE : B_GATE + R_GATE, :] = get_rows(gs_ref, dev, R_GATE)
            stage_ref[B_UP : B_UP + R_GATE, :] = get_rows(us_ref, dev, R_GATE)
            (keep_b_ref if keep_it else send_b_ref)[slot] = stage_ref[...].astype(BF16)
        return carry

    lax.fori_loop(0, CHIPS, spread, 0)


def ffn(where, a_own, a_other, b_own, b_other, x_t, o_t, cot_t, gain):
    seqs = x_t.shape[0]
    cols_all = seqs * SEQ
    vmem = pl.BlockSpec(memory_space=pltpu.VMEM)
    return pl.pallas_call(
        ffn_kernel,
        in_specs=[pl.BlockSpec(memory_space=pltpu.SMEM)] + [vmem] * 8,
        out_specs=[vmem] * 8,
        out_shape=[
            jax.ShapeDtypeStruct((seqs, D, SEQ), BF16),
            jax.ShapeDtypeStruct((seqs, D, SEQ), F32),
            jax.ShapeDtypeStruct((seqs, D, SEQ), BF16),
            jax.ShapeDtypeStruct((D, 1), F32),
            jax.ShapeDtypeStruct((CHIPS, ROWS_G, 128), BF16),
            jax.ShapeDtypeStruct((CHIPS, ROWS_G, 128), BF16),
            jax.ShapeDtypeStruct((CHIPS, ROWS_B, 128), BF16),
            jax.ShapeDtypeStruct((CHIPS, ROWS_B, 128), BF16),
        ],
        scratch_shapes=[
            pltpu.VMEM((2 * CHIPS * R_GATE, 128), F32),
            pltpu.VMEM((2 * CHIPS * R_GATE, 128), F32),
            pltpu.VMEM((2 * CHIPS * R_DOWN, 128), F32),
            pltpu.VMEM((2 * CHIPS * R_OUT, 128), F32),
            pltpu.VMEM((D, FF), BF16),
            pltpu.VMEM((D, FF), BF16),
            pltpu.VMEM((FF, D), BF16),
            pltpu.VMEM((D, D), BF16),
            pltpu.VMEM((D, cols_all), F32),
            pltpu.VMEM((D, cols_all), BF16),
            pltpu.VMEM((D, cols_all), BF16),
            pltpu.VMEM((D, cols_all), F32),
            pltpu.VMEM((1, cols_all), F32),
            pltpu.VMEM((ROWS_B, 128), F32),
        ],
        compiler_params=pltpu.CompilerParams(vmem_limit_bytes=63 * 2**20),
        cost_estimate=pl.CostEstimate(
            flops=25 * 10**9, bytes_accessed=30 * 10**6, transcendentals=2 * 10**6
        ),
        name="ffn",
    )(where, a_own, a_other, b_own, b_other, x_t, o_t, cot_t, gain)


def attn_bwd_kernel(
    cos_ref, sin_ref, q_t_ref, k_t_ref, v_t_ref, p_ref, o_t_ref, do_t_ref, *rest
):
    dqkv_ref, dq_ref, v_ref = rest[-3:]
    for group in range(KV_HEADS):
        v_ref[group] = v_t_ref[0, group * HEAD : (group + 1) * HEAD, :].astype(F32).T.astype(BF16)

    def group_step(group, carry):
        kv_rows = pl.ds(pl.multiple_of(group * HEAD, HEAD), HEAD)
        dk = [jnp.zeros((HEAD, HALF), F32) for _ in range(2)]
        dv = [jnp.zeros((HEAD, HALF), F32) for _ in range(2)]
        for member in range(HEADS // KV_HEADS):
            head = group * (HEADS // KV_HEADS) + member
            rows = pl.ds(pl.multiple_of(head * HEAD, HEAD), HEAD)
            for block in range(2):
                cols = slice(block * HALF, (block + 1) * HALF)
                keys = slice(0, (block + 1) * HALF)
                do_t = do_t_ref[0, rows, cols]
                q_t = q_t_ref[0, rows, cols]
                p_t = p_ref[0, head, keys, cols]
                row_sum = jnp.sum(
                    do_t.astype(F32) * o_t_ref[0, rows, cols].astype(F32), axis=0, keepdims=True
                )
                dp_t = mm(v_ref[group, keys, :], do_t)
                ds_t = (p_t.astype(F32) * (dp_t - row_sum)).astype(BF16)
                dq_ref[rows, cols] = mm(k_t_ref[0, kv_rows, keys], ds_t) * 0.125
                dk_new = mm(q_t, ds_t, NT)
                dv_new = mm(do_t, p_t, NT)
                for part in range(block + 1):
                    at = slice(part * HALF, (part + 1) * HALF)
                    dk[part] += dk_new[:, at]
                    dv[part] += dv_new[:, at]
        dq_ref[pl.ds(pl.multiple_of(D + group * HEAD, HEAD), HEAD), :] = jnp.concatenate(dk, axis=1)
        dqkv_ref[pl.ds(pl.multiple_of(D + KVW + group * HEAD, HEAD), HEAD), :] = jnp.concatenate(
            dv, axis=1
        ).astype(BF16)
        return carry

    lax.fori_loop(0, KV_HEADS, group_step, 0)
    dqkv_ref[: D + KVW] = rope_rows(
        dq_ref[...], cos_ref[0], sin_ref[0], HEADS + KV_HEADS, -1
    ).astype(BF16)


def attn_bwd(seq, args, after):
    return pl.pallas_call(
        attn_bwd_kernel,
        grid=(1,),
        in_specs=[
            seq_spec((32, SEQ), seq),
            seq_spec((32, SEQ), seq),
            seq_spec((D, SEQ), seq),
            seq_spec((KVW, SEQ), seq),
            seq_spec((KVW, SEQ), seq),
            seq_spec((HEADS, SEQ, SEQ), seq),
            seq_spec((D, SEQ), seq),
            seq_spec((D, SEQ), seq),
        ]
        + [pl.BlockSpec(memory_space=pl.ANY)] * len(after),
        out_specs=whole_spec((QKV, SEQ)),
        out_shape=jax.ShapeDtypeStruct((QKV, SEQ), BF16),
        scratch_shapes=[
            pltpu.VMEM((D + KVW, SEQ), F32),
            pltpu.VMEM((KV_HEADS, SEQ, HEAD), BF16),
        ],
        compiler_params=pltpu.CompilerParams(vmem_limit_bytes=40 * 2**20),
        cost_estimate=pl.CostEstimate(flops=8 * 10**9, bytes_accessed=8 * 10**6, transcendentals=0),
        name="attn_bwd",
    )(*args, *after)


def qkv_bwd_kernel(
    where_ref, w_ref, gain_ref, dgain_two_ref, x_ref, h_t_ref, dx1_ref, dqkv0_ref, dqkv1_ref, *rest
):
    gx_ref, send_ref, keep_ref, dw_ref, dgain_ref, qs_ref, ks_ref, vs_ref, gs_ref, stage_ref = rest[-10:]
    dw = jnp.zeros((D, QKV), F32)
    dgain = jnp.zeros((D, 1), F32)
    for seq, dqkv_ref in enumerate((dqkv0_ref, dqkv1_ref)):
        dqkv = dqkv_ref[...]
        dh = mm(w_ref[...], dqkv)
        dw += mm(h_t_ref[seq], dqkv, NT)
        x = x_ref[seq].astype(F32)
        inv = lax.rsqrt(jnp.mean(x * x, axis=0, keepdims=True) + EPSILON)
        normed = x * inv
        dn = dh * gain_ref[:D]
        gx_ref[seq] = dx1_ref[seq] + inv * (
            dn - normed * jnp.mean(dn * normed, axis=0, keepdims=True)
        )
        dgain += jnp.sum(dh * normed, axis=1, keepdims=True)
    dw_ref[...] = dw
    dgain_ref[:D] = dgain
    dgain_ref[D:] = dgain_two_ref[...]
    join_square(qs_ref, dw_ref)
    for half in range(2):
        at = D + 96 * half
        ks_ref[pl.ds(half, D, stride=2), :96] = dw_ref[:, at : at + 96]
        vs_ref[pl.ds(half, D, stride=2), :96] = dw_ref[:, at + KVW : at + KVW + 96]
    for lane in range(9):
        gs_ref[:, lane : lane + 1] = dgain_ref[pl.ds(lane, 2 * CHIPS, stride=9), :]
    core = where_ref[0]
    stage_ref[...] = jnp.zeros_like(stage_ref)

    def spread(slot, carry):
        chip = chip_of(slot, where_ref, False, 1)
        for keep_it in range(2):
            dev = chip * 2 + (core if keep_it else 1 - core)
            stage_ref[Q_QUERY : Q_QUERY + R_OUT, :] = get_rows(qs_ref, dev, R_OUT)
            stage_ref[Q_KEY : Q_KEY + R_KEY, :] = get_rows(ks_ref, dev, R_KEY)
            stage_ref[Q_VALUE : Q_VALUE + R_KEY, :] = get_rows(vs_ref, dev, R_KEY)
            stage_ref[Q_GAIN : Q_GAIN + 1, :] = get_rows(gs_ref, dev, 1)
            (keep_ref if keep_it else send_ref)[slot] = stage_ref[...].astype(BF16)
        return carry

    lax.fori_loop(0, CHIPS, spread, 0)


def qkv_bwd(args, after):
    seqs = args[4].shape[0]
    vmem = pl.BlockSpec(memory_space=pltpu.VMEM)
    return pl.pallas_call(
        qkv_bwd_kernel,
        in_specs=[pl.BlockSpec(memory_space=pltpu.SMEM)]
        + [vmem] * (len(args) - 1)
        + [pl.BlockSpec(memory_space=pl.ANY)] * len(after),
        out_specs=[vmem] * 3,
        out_shape=[
            jax.ShapeDtypeStruct((seqs, D, SEQ), F32),
            jax.ShapeDtypeStruct((CHIPS, ROWS_Q, 128), BF16),
            jax.ShapeDtypeStruct((CHIPS, ROWS_Q, 128), BF16),
        ],
        scratch_shapes=[
            pltpu.VMEM((D, QKV), F32),
            pltpu.VMEM((2 * D, 1), F32),
            pltpu.VMEM((2 * CHIPS * R_OUT, 128), F32),
            pltpu.VMEM((2 * CHIPS * R_KEY, 128), F32),
            pltpu.VMEM((2 * CHIPS * R_KEY, 128), F32),
            pltpu.VMEM((2 * CHIPS, 128), F32),
            pltpu.VMEM((ROWS_Q, 128), F32),
        ],
        compiler_params=pltpu.CompilerParams(vmem_limit_bytes=40 * 2**20),
        cost_estimate=pl.CostEstimate(flops=8 * 10**9, bytes_accessed=12 * 10**6, transcendentals=0),
        name="qkv_bwd",
    )(*args, *after)


def pairs(axis, step):
    out = []
    for x in range(4):
        for y in range(4):
            for z in range(4):
                for core in range(2):
                    to = {"x": x, "y": y, "z": z, "c": core}
                    to[axis] = (to[axis] + step) % (2 if axis == "c" else 4)
                    me = ((x * 4 + y) * 4 + z) * 2 + core
                    out.append((me, ((to["x"] * 4 + to["y"]) * 4 + to["z"]) * 2 + to["c"]))
    return out


def hop(v, axis, step):
    return lax.ppermute(v, "dp", pairs(axis, step))


def gather_near(v, axis):
    far = hop(v, axis, 2)
    return jnp.stack([v, hop(v, axis, 1), far, hop(v, axis, 3)])


def join_kernel(own_ref, *refs):
    ins, (a_ref, b_ref) = refs[:-2], refs[-2:]
    for at, out_ref, (left, right, far_left, far_right) in (
        (slice(0, ROWS_A), a_ref, ins[:4]),
        (slice(ROWS_A, ROWS_A + ROWS_B), b_ref, ins[4:]),
    ):
        out_ref[0] = own_ref[:, at, :]
        out_ref[1] = left[...]
        out_ref[2, :2] = far_left[...]
        out_ref[2, 2:] = far_right[...]
        out_ref[3] = right[...]


def gather_both(ab):
    ins = []
    for v, axis in ((ab[:, :ROWS_A], "y"), (ab[:, ROWS_A:], "z")):
        left = hop(v, axis, 1)
        right = hop(v, axis, 3)
        ins += [left, right, hop(left[:2], axis, 1), hop(right[2:], axis, 3)]
    vmem = pl.BlockSpec(memory_space=pltpu.VMEM)
    return pl.pallas_call(
        join_kernel,
        in_specs=[vmem] * 9,
        out_specs=[vmem] * 2,
        out_shape=[
            jax.ShapeDtypeStruct((4, 4, ROWS_A, 128), BF16),
            jax.ShapeDtypeStruct((4, 4, ROWS_B, 128), BF16),
        ],
        name="join",
    )(ab, *ins)


def cut_kernel(la_ref, ra_ref, lb_ref, rb_ref, *outs):
    for out, ref, at in zip(outs, (la_ref, ra_ref, lb_ref, rb_ref), (0, 2, 0, 2)):
        out[...] = ref[at : at + 2]


def gather_wide(a, b):
    near = [hop(a, "z", 1), hop(a, "z", 3), hop(b, "y", 1), hop(b, "y", 3)]
    vmem = pl.BlockSpec(memory_space=pltpu.VMEM)
    halves = pl.pallas_call(
        cut_kernel,
        in_specs=[vmem] * 4,
        out_specs=[vmem] * 4,
        out_shape=[
            jax.ShapeDtypeStruct((2, 4, rows, 128), BF16) for rows in (ROWS_A, ROWS_A, ROWS_B, ROWS_B)
        ],
        name="cut",
    )(*near)
    out = []
    for v, axis, (left, right), (far_left, far_right) in (
        (a, "z", near[:2], halves[:2]),
        (b, "y", near[2:], halves[2:]),
    ):
        far = [hop(far_left, axis, 1), hop(far_right, axis, 3)]
        out.append(jnp.concatenate([v, left] + far + [right]).reshape(CHIPS, -1, 128))
    return out


def sum_near(v, axis):
    low = v[1:].astype(BF16)
    got = [hop(low[k - 1], axis, k) for k in (2, 1, 3)]
    total = v[0].astype(F32)
    for piece in got:
        total = total + piece.astype(F32)
    return total


def ring_far(v, axis):
    cut = v.shape[1] // 2
    far = v[2].astype(BF16)
    from_left = hop(far[:cut], axis, 1).astype(F32)
    from_right = hop(far[cut:], axis, 3).astype(F32)
    ahead = jnp.concatenate([v[1][:cut] + from_left, v[1][cut:]]).astype(BF16)
    behind = jnp.concatenate([v[3][:cut], v[3][cut:] + from_right]).astype(BF16)
    return v[0], ahead, behind


def ring_near(parts, axis):
    own, ahead, behind = parts
    return own + hop(ahead, axis, 1).astype(F32) + hop(behind, axis, 3).astype(F32)


def on_device(
    tokens, positions, norm_gains, w_query, w_key, w_value, w_out, w_gate, w_up, w_down, cotangent
):
    me = lax.axis_index("dp").astype(jnp.int32)
    where = jnp.stack([me % 2, me // 32, (me // 8) % 4, (me // 2) % 4])
    seqs = tokens.shape[0]
    x_t = jnp.swapaxes(tokens, 1, 2)
    cot_t = jnp.swapaxes(cotangent, 1, 2)

    packed = pack(
        [
            lane_rows(jnp.concatenate([w_query, w_out]), 18, 288),
            jnp.concatenate([w_key, w_value]).reshape(18, 96),
            norm_gains.reshape(1, 9),
            lane_rows(w_down, 12, D),
            jnp.concatenate([w_gate, w_up]).reshape(2 * R_GATE, 128),
        ]
    )
    ab = gather_near(packed, "x")
    a, b = gather_both(ab)
    a_own, b_own = gather_wide(a, b)
    a_other = hop(a_own, "c", 1)
    b_other = hop(b_own, "c", 1)

    freqs = 100000.0 ** (-(jnp.arange(HEAD // 2, dtype=F32) * 2.0 / HEAD))
    angles = positions.astype(F32)[:, None, :] * freqs[None, :, None]
    cos_t = jnp.cos(angles)
    sin_t = jnp.sin(angles)
    fresh = (positions[:, 1:] != positions[:, :-1] + 1).astype(jnp.int32)
    docs = jnp.cumsum(jnp.pad(fresh, ((0, 0), (1, 0))), axis=1)

    wqkv, gain, h_t, q_t, k_t, v_t, p, o_t = attn_fwd(
        where, a_own, a_other, x_t, cos_t, sin_t, docs[:, None, :], docs[:, :, None]
    )
    y_t, dx1, do_t, dgain_two, send_g, keep_g, send_b, keep_b = ffn(
        where, a_own, a_other, b_own, b_other, x_t, o_t, cot_t, gain
    )
    got_g = hop(send_g, "c", 1)
    got_b = hop(send_b, "c", 1)
    args = [cos_t, sin_t, q_t, k_t, v_t, p, o_t, do_t]
    dqkv0 = attn_bwd(0, args, [])
    sum_g = (keep_g.astype(F32) + got_g.astype(F32)).reshape(4, 4, 4, ROWS_G, 128)
    sum_b = (keep_b.astype(F32) + got_b.astype(F32)).reshape(4, 4, 4, ROWS_B, 128)
    dqkv1 = attn_bwd(1, args, [sum_g, sum_b])
    part_g = ring_far(sum_g, "z")
    part_b = ring_far(sum_b, "y")
    gx_t, send_q, keep_q = qkv_bwd(
        [where, wqkv, gain, dgain_two, x_t, h_t, dx1, dqkv0, dqkv1], part_g[1:] + part_b[1:]
    )
    got_q = hop(send_q, "c", 1)
    sum_g = ring_near(part_g, "z")
    sum_b = ring_near(part_b, "y")
    sum_q = (keep_q.astype(F32) + got_q.astype(F32)).reshape(4, 4, 4, ROWS_Q, 128)
    sum_q = sum_near(sum_q, "z")
    sum_b = sum_near(sum_b, "z")
    sum_a = sum_near(jnp.concatenate([sum_g, sum_q], axis=2), "y")
    final = sum_near(jnp.concatenate([sum_a, sum_b], axis=1), "x")
    fg = final[:ROWS_G]
    fq = final[ROWS_G : ROWS_G + ROWS_Q]
    fb = final[ROWS_G + ROWS_Q :]
    return (
        jnp.swapaxes(y_t, 1, 2),
        jnp.swapaxes(gx_t, 1, 2),
        take_lanes(fq[Q_GAIN : Q_GAIN + 1], 1, 9),
        take_lanes(fq[Q_QUERY : Q_QUERY + R_OUT], 9, 288),
        take_lanes(fq[Q_KEY : Q_KEY + R_KEY], 9, 96),
        take_lanes(fq[Q_VALUE : Q_VALUE + R_KEY], 9, 96),
        take_lanes(fg[G_OUT : G_OUT + R_OUT], 9, 288),
        fb[B_GATE : B_GATE + R_GATE].reshape(-1),
        fb[B_UP : B_UP + R_GATE].reshape(-1),
        take_lanes(fg[G_DOWN : G_DOWN + R_DOWN], 12, D),
    )


def solution(mesh):
    flat = P("dp")
    cube = P("dp", None, None)
    return jax.shard_map(
        on_device,
        mesh=mesh,
        in_specs=(cube, P("dp", None)) + (flat,) * 8 + (cube,),
        out_specs=(cube, cube) + (flat,) * 8,
        check_vma=False,
    )
```

```python
import functools

import jax
import jax.numpy as jnp
from jax import lax
from jax.sharding import PartitionSpec as P
from jax.experimental import pallas as pl
from jax.experimental.pallas import tpu as pltpu

D = 576
HEADS = 9
KV_HEADS = 3
HEAD = 64
FF = 1536
SEQ = 512
KVW = KV_HEADS * HEAD
QKV = D + 2 * KVW
HALF = SEQ // 2

EPSILON = 1e-05
NEG_FILL = -1e30

F32 = jnp.float32
BF16 = jnp.bfloat16

CHIPS = 64
R_GATE = 54
R_DOWN = 60
R_OUT = 27
R_KEY = 9
F_GATE, F_UP, F_DOWN, F_OUT, ROWS_F = 0, 54, 112, 172, 208
B_GATE, B_UP, ROWS_B = 0, 54, 112
G_DOWN, G_OUT, ROWS_G = 0, 60, 96
Q_QUERY, Q_KEY, Q_VALUE, Q_GAIN, ROWS_Q = 0, 27, 36, 45, 48

NN = (((1,), (0,)), ((), ()))
NT = (((1,), (1,)), ((), ()))
TN = (((0,), (0,)), ((), ()))


def mm(a, b, dims=NN):
    return lax.dot_general(a, b, dims, preferred_element_type=F32)


def whole_spec(shape):
    zeros = (0,) * len(shape)
    return pl.BlockSpec(shape, lambda i: zeros)


def seq_spec(shape, at=None):
    zeros = (0,) * len(shape)
    return pl.BlockSpec((1,) + shape, lambda i: (i if at is None else at,) + zeros)


def chip_of(slot, where_ref, swap):
    one, two, three = slot // 16, (slot // 4) % 4, slot % 4
    kz, ky = (two, one) if swap else (one, two)
    x = (where_ref[1] + three) % 4
    y = (where_ref[2] + ky) % 4
    z = (where_ref[3] + kz) % 4
    return (x * 4 + y) * 4 + z


def put_rows(ref, dev, rows, val):
    ref[pl.ds(dev * rows, rows), :] = val


def get_rows(ref, dev, rows):
    return ref[pl.ds(dev * rows, rows), :]


def split_square(ref):
    parts = []
    for half in range(2):
        for j in range(3):
            piece = ref[pl.ds(3 * half + j, D, stride=6), :]
            parts.append(piece if j < 2 else piece[:, :32])
    return parts


def join_square(ref, val_ref):
    for half in range(2):
        for j in range(3):
            width = 128 if j < 2 else 32
            at = 288 * half + 128 * j
            ref[pl.ds(3 * half + j, D, stride=6), :width] = val_ref[:, at : at + width]


def pack_kernel(wqo, wkv, gn, wd, wgu, f_ref, q_ref, f_stage_ref, q_stage_ref):
    f_stage_ref[...] = jnp.zeros_like(f_stage_ref)
    q_stage_ref[...] = jnp.zeros_like(q_stage_ref)
    square = wqo[...].astype(F32)
    thin = wkv[...].astype(F32)
    for ref, at, val in (
        (q_stage_ref, Q_QUERY, square[:R_OUT]),
        (q_stage_ref, Q_KEY, thin[:R_KEY]),
        (q_stage_ref, Q_VALUE, thin[R_KEY:]),
        (q_stage_ref, Q_GAIN, gn[...].astype(F32)),
        (f_stage_ref, F_GATE, wgu[...].astype(F32)),
        (f_stage_ref, F_DOWN, wd[...].astype(F32)),
        (f_stage_ref, F_OUT, square[R_OUT:]),
    ):
        ref[at : at + val.shape[0], : val.shape[1]] = val
    f_ref[...] = f_stage_ref[...].astype(BF16)
    q_ref[...] = q_stage_ref[...].astype(BF16)


def pack(pieces):
    vmem = pl.BlockSpec(memory_space=pltpu.VMEM)
    return pl.pallas_call(
        pack_kernel,
        in_specs=[vmem] * 5,
        out_specs=[vmem] * 2,
        out_shape=[
            jax.ShapeDtypeStruct((ROWS_F, 128), BF16),
            jax.ShapeDtypeStruct((ROWS_Q, 128), BF16),
        ],
        scratch_shapes=[pltpu.VMEM((ROWS_F, 128), F32), pltpu.VMEM((ROWS_Q, 128), F32)],
        name="pack",
    )(*pieces)


def lane_rows(v, rows, width):
    v = v.reshape(rows, width)
    full = -(-width // 128) * 128
    v = jnp.pad(v, ((0, 0), (0, full - width)))
    return v.reshape(rows * full // 128, 128)


def take_lanes(v, rows, width):
    full = -(-width // 128) * 128
    return v.reshape(rows, full)[:, :width].reshape(-1)


def rope_rows(v, cos_t, sin_t, heads, sign):
    out = []
    for head in range(heads):
        lo = v[head * HEAD : head * HEAD + 32]
        hi = v[head * HEAD + 32 : head * HEAD + 64]
        if sign > 0:
            out += [lo * cos_t - hi * sin_t, hi * cos_t + lo * sin_t]
        else:
            out += [lo * cos_t + hi * sin_t, hi * cos_t - lo * sin_t]
    return jnp.concatenate(out, axis=0)


def attn_fwd_kernel(
    pack_ref, x_ref, cos_ref, sin_ref, docr_ref, docc_ref,
    wqkv_ref, gain_ref, h_t_ref, q_t_ref, k_t_ref, v_t_ref, p_ref, o_t_ref,
    qs_ref, ks_ref, vs_ref, gs_ref, w_t_ref, bias_ref, k_ref,
):
    @pl.when(pl.program_id(0) == 0)
    def _():
        def squeeze(dev, carry):
            val = pack_ref[dev].astype(F32)
            put_rows(qs_ref, dev, R_OUT, val[Q_QUERY : Q_QUERY + R_OUT])
            put_rows(ks_ref, dev, R_KEY, val[Q_KEY : Q_KEY + R_KEY])
            put_rows(vs_ref, dev, R_KEY, val[Q_VALUE : Q_VALUE + R_KEY])
            put_rows(gs_ref, dev, 1, val[Q_GAIN : Q_GAIN + 1])
            return carry

        lax.fori_loop(0, 2 * CHIPS, squeeze, 0)
        parts = split_square(qs_ref)
        for ref in (ks_ref, vs_ref):
            for half in range(2):
                parts.append(ref[pl.ds(half, D, stride=2), :][:, :96])
        whole = jnp.concatenate(parts, axis=1)
        wqkv_ref[...] = whole.astype(BF16)
        w_t_ref[...] = whole.T.astype(BF16)
        for lane in range(9):
            gain_ref[pl.ds(lane, 2 * CHIPS, stride=9), :] = gs_ref[:, lane : lane + 1]

    x = x_ref[0].astype(F32)
    inv = lax.rsqrt(jnp.mean(x * x, axis=0, keepdims=True) + EPSILON)
    h_t = ((x * inv) * gain_ref[:D]).astype(BF16)
    h_t_ref[0] = h_t
    cos_t = cos_ref[0]
    sin_t = sin_ref[0]
    q_t = mm(w_t_ref[:D], h_t)
    q_t_ref[0] = rope_rows(q_t, cos_t, sin_t, HEADS, 1).astype(BF16) * 0.125
    k_t = rope_rows(mm(w_t_ref[D : D + KVW], h_t), cos_t, sin_t, KV_HEADS, 1).astype(BF16)
    k_t_ref[0] = k_t
    for group in range(KV_HEADS):
        k_ref[group] = k_t[group * HEAD : (group + 1) * HEAD].astype(F32).T.astype(BF16)
    v_t_ref[0] = mm(w_t_ref[D + KVW :], h_t).astype(BF16)
    key_at = lax.broadcasted_iota(jnp.int32, (SEQ, SEQ), 0)
    query_at = lax.broadcasted_iota(jnp.int32, (SEQ, SEQ), 1)
    same = docc_ref[0] == docr_ref[0]
    bias_ref[...] = jnp.where(same & (key_at <= query_at), 0.0, NEG_FILL)

    def group_step(group, carry):
        kv_rows = pl.ds(pl.multiple_of(group * HEAD, HEAD), HEAD)
        for member in range(HEADS // KV_HEADS):
            head = group * (HEADS // KV_HEADS) + member
            rows = pl.ds(pl.multiple_of(head * HEAD, HEAD), HEAD)
            for block in range(2):
                cols = slice(block * HALF, (block + 1) * HALF)
                keys = slice(0, (block + 1) * HALF)
                s_t = mm(k_ref[group, keys, :], q_t_ref[0, rows, cols]) + bias_ref[keys, cols]
                peak = jnp.max(s_t, axis=0, keepdims=True)
                e_t = jnp.exp(s_t - peak)
                scale = 1.0 / jnp.sum(e_t, axis=0, keepdims=True)
                p_t = (e_t * scale).astype(BF16)
                p_ref[0, head, keys, cols] = p_t
                o_t_ref[0, rows, cols] = mm(v_t_ref[0, kv_rows, keys], p_t).astype(BF16)
        return carry

    lax.fori_loop(0, KV_HEADS, group_step, 0)


def attn_fwd(pack_q, x_t, cos_t, sin_t, doc_row, doc_col):
    seqs = x_t.shape[0]
    out = [
        ((D, QKV), BF16, False),
        ((2 * D, 1), F32, False),
        ((D, SEQ), BF16, True),
        ((D, SEQ), BF16, True),
        ((KVW, SEQ), BF16, True),
        ((KVW, SEQ), BF16, True),
        ((HEADS, SEQ, SEQ), BF16, True),
        ((D, SEQ), BF16, True),
    ]
    return pl.pallas_call(
        attn_fwd_kernel,
        grid=(seqs,),
        in_specs=[
            whole_spec((2 * CHIPS, ROWS_Q, 128)),
            seq_spec((D, SEQ)),
            seq_spec((32, SEQ)),
            seq_spec((32, SEQ)),
            seq_spec((1, SEQ)),
            seq_spec((SEQ, 1)),
        ],
        out_specs=[seq_spec(s) if per else whole_spec(s) for s, _, per in out],
        out_shape=[jax.ShapeDtypeStruct(((seqs,) + s) if per else s, t) for s, t, per in out],
        scratch_shapes=[
            pltpu.VMEM((2 * CHIPS * R_OUT, 128), F32),
            pltpu.VMEM((2 * CHIPS * R_KEY, 128), F32),
            pltpu.VMEM((2 * CHIPS * R_KEY, 128), F32),
            pltpu.VMEM((2 * CHIPS, 128), F32),
            pltpu.VMEM((QKV, D), BF16),
            pltpu.VMEM((SEQ, SEQ), F32),
            pltpu.VMEM((KV_HEADS, SEQ, HEAD), BF16),
        ],
        compiler_params=pltpu.CompilerParams(vmem_limit_bytes=63 * 2**20),
        cost_estimate=pl.CostEstimate(
            flops=8 * 10**9, bytes_accessed=20 * 10**6, transcendentals=5 * 10**6
        ),
        name="attn_fwd",
    )(pack_q, x_t, cos_t, sin_t, doc_row, doc_col)


CHUNK = 256
CHUNKS = FF // CHUNK


def ffn_kernel(
    where_ref, pack_ref, x_ref, o_t_ref, cot_ref, gain_ref,
    y_ref, dx1_ref, do_t_ref, dgain_ref, send_g_ref, keep_g_ref, send_b_ref, keep_b_ref,
    gs_ref, us_ref, ds_ref, os_ref, wg_ref, wu_ref, wd_ref, wo_ref,
    acc_ref, h_t_ref, gb_ref, dh_ref, inv_ref, stage_ref,
):
    seqs = x_ref.shape[0]
    core = where_ref[0]

    def squeeze(dev, carry):
        val = pack_ref[dev].astype(F32)
        put_rows(gs_ref, dev, R_GATE, val[F_GATE : F_GATE + R_GATE])
        put_rows(us_ref, dev, R_GATE, val[F_UP : F_UP + R_GATE])
        put_rows(ds_ref, dev, R_DOWN, val[F_DOWN : F_DOWN + R_DOWN])
        put_rows(os_ref, dev, R_OUT, val[F_OUT : F_OUT + R_OUT])
        return carry

    lax.fori_loop(0, 2 * CHIPS, squeeze, 0)
    wo_ref[...] = jnp.concatenate(split_square(os_ref), axis=1).astype(BF16)
    for j in range(12):
        cols = slice(j * 128, (j + 1) * 128)
        wg_ref[:, cols] = gs_ref[pl.ds(j, D, stride=12), :].astype(BF16)
        wu_ref[:, cols] = us_ref[pl.ds(j, D, stride=12), :].astype(BF16)
    for j in range(5):
        width = min(128, D - j * 128)
        wd_ref[:, j * 128 : j * 128 + width] = ds_ref[pl.ds(j, FF, stride=5), :][:, :width].astype(BF16)

    gain = gain_ref[D:]
    for seq in range(seqs):
        cols = slice(seq * SEQ, (seq + 1) * SEQ)
        x1 = x_ref[seq].astype(F32) + mm(wo_ref[...], o_t_ref[seq], TN)
        inv = lax.rsqrt(jnp.mean(x1 * x1, axis=0, keepdims=True) + EPSILON)
        normed = x1 * inv
        acc_ref[:, cols] = x1
        inv_ref[:, cols] = inv
        dx1_ref[seq] = normed
        h_t_ref[:, cols] = (normed * gain).astype(BF16)
        gb_ref[:, cols] = cot_ref[seq].astype(BF16)
    dh_ref[...] = jnp.zeros_like(dh_ref)

    def chunk_step(chunk, carry):
        cols = pl.ds(pl.multiple_of(chunk * CHUNK, CHUNK), CHUNK)
        wg = wg_ref[:, cols]
        wu = wu_ref[:, cols]
        wd = wd_ref[cols, :]
        h_t = h_t_ref[...]
        gb = gb_ref[...]
        a = mm(wg, h_t, TN)
        b = mm(wu, h_t, TN)
        dm = mm(wd, gb)
        sg = 1.0 / (1.0 + jnp.exp(-a))
        silu = a * sg
        m = (silu * b).astype(BF16)
        da = (dm * b * sg * (1.0 + a * (1.0 - sg))).astype(BF16)
        db = (dm * silu).astype(BF16)
        acc_ref[...] += mm(wd, m, TN)
        dh_ref[...] += mm(wg, da) + mm(wu, db)
        dwg = mm(h_t, da, NT)
        dwu = mm(h_t, db, NT)
        dwd = mm(m, gb, NT)
        for j in range(CHUNK // 128):
            lane = slice(j * 128, (j + 1) * 128)
            at = chunk * (CHUNK // 128) + j
            gs_ref[pl.ds(at, D, stride=12), :] = dwg[:, lane]
            us_ref[pl.ds(at, D, stride=12), :] = dwu[:, lane]
        for j in range(5):
            width = min(128, D - j * 128)
            ds_ref[pl.ds(chunk * CHUNK * 5 + j, CHUNK, stride=5), :width] = dwd[
                :, j * 128 : j * 128 + width
            ]
        return carry

    lax.fori_loop(0, CHUNKS, chunk_step, 0)

    dgain = jnp.zeros((D, 1), F32)
    dwo = jnp.zeros((D, D), F32)
    for seq in range(seqs):
        cols = slice(seq * SEQ, (seq + 1) * SEQ)
        y_ref[seq] = acc_ref[:, cols].astype(BF16)
        dh = dh_ref[:, cols]
        normed = dx1_ref[seq]
        dgain += jnp.sum(dh * normed, axis=1, keepdims=True)
        dn = dh * gain
        dx1 = cot_ref[seq] + inv_ref[:, cols] * (
            dn - normed * jnp.mean(dn * normed, axis=0, keepdims=True)
        )
        dx1_ref[seq] = dx1
        low = dx1.astype(BF16)
        dwo += mm(o_t_ref[seq], low, NT)
        do_t_ref[seq] = mm(wo_ref[...], low).astype(BF16)
    dgain_ref[...] = dgain
    dh_ref[:, :D] = dwo
    join_square(os_ref, dh_ref)

    stage_ref[...] = jnp.zeros_like(stage_ref)

    def spread(slot, carry):
        for keep_it in range(2):
            chip = chip_of(slot, where_ref, False)
            dev = chip * 2 + (core if keep_it else 1 - core)
            stage_ref[G_DOWN : G_DOWN + R_DOWN, :] = get_rows(ds_ref, dev, R_DOWN)
            stage_ref[G_OUT : G_OUT + R_OUT, :] = get_rows(os_ref, dev, R_OUT)
            (keep_g_ref if keep_it else send_g_ref)[slot] = stage_ref[:ROWS_G].astype(BF16)
            chip = chip_of(slot, where_ref, True)
            dev = chip * 2 + (core if keep_it else 1 - core)
            stage_ref[B_GATE : B_GATE + R_GATE, :] = get_rows(gs_ref, dev, R_GATE)
            stage_ref[B_UP : B_UP + R_GATE, :] = get_rows(us_ref, dev, R_GATE)
            (keep_b_ref if keep_it else send_b_ref)[slot] = stage_ref[...].astype(BF16)
        return carry

    lax.fori_loop(0, CHIPS, spread, 0)


def ffn(where, pack_f, x_t, o_t, cot_t, gain):
    seqs = x_t.shape[0]
    cols_all = seqs * SEQ
    vmem = pl.BlockSpec(memory_space=pltpu.VMEM)
    return pl.pallas_call(
        ffn_kernel,
        in_specs=[pl.BlockSpec(memory_space=pltpu.SMEM)] + [vmem] * 5,
        out_specs=[vmem] * 8,
        out_shape=[
            jax.ShapeDtypeStruct((seqs, D, SEQ), BF16),
            jax.ShapeDtypeStruct((seqs, D, SEQ), F32),
            jax.ShapeDtypeStruct((seqs, D, SEQ), BF16),
            jax.ShapeDtypeStruct((D, 1), F32),
            jax.ShapeDtypeStruct((CHIPS, ROWS_G, 128), BF16),
            jax.ShapeDtypeStruct((CHIPS, ROWS_G, 128), BF16),
            jax.ShapeDtypeStruct((CHIPS, ROWS_B, 128), BF16),
            jax.ShapeDtypeStruct((CHIPS, ROWS_B, 128), BF16),
        ],
        scratch_shapes=[
            pltpu.VMEM((2 * CHIPS * R_GATE, 128), F32),
            pltpu.VMEM((2 * CHIPS * R_GATE, 128), F32),
            pltpu.VMEM((2 * CHIPS * R_DOWN, 128), F32),
            pltpu.VMEM((2 * CHIPS * R_OUT, 128), F32),
            pltpu.VMEM((D, FF), BF16),
            pltpu.VMEM((D, FF), BF16),
            pltpu.VMEM((FF, D), BF16),
            pltpu.VMEM((D, D), BF16),
            pltpu.VMEM((D, cols_all), F32),
            pltpu.VMEM((D, cols_all), BF16),
            pltpu.VMEM((D, cols_all), BF16),
            pltpu.VMEM((D, cols_all), F32),
            pltpu.VMEM((1, cols_all), F32),
            pltpu.VMEM((ROWS_B, 128), F32),
        ],
        compiler_params=pltpu.CompilerParams(vmem_limit_bytes=63 * 2**20),
        cost_estimate=pl.CostEstimate(
            flops=25 * 10**9, bytes_accessed=30 * 10**6, transcendentals=2 * 10**6
        ),
        name="ffn",
    )(where, pack_f, x_t, o_t, cot_t, gain)


def attn_bwd_kernel(
    handed, cos_ref, sin_ref, q_t_ref, k_t_ref, v_t_ref, p_ref, o_t_ref, do_t_ref, *rest
):
    dqkv_ref = rest[handed]
    dq_ref, v_ref = rest[-2:]
    for group in range(KV_HEADS):
        v_ref[group] = v_t_ref[0, group * HEAD : (group + 1) * HEAD, :].astype(F32).T.astype(BF16)

    def group_step(group, carry):
        kv_rows = pl.ds(pl.multiple_of(group * HEAD, HEAD), HEAD)
        dk = [jnp.zeros((HEAD, HALF), F32) for _ in range(2)]
        dv = [jnp.zeros((HEAD, HALF), F32) for _ in range(2)]
        for member in range(HEADS // KV_HEADS):
            head = group * (HEADS // KV_HEADS) + member
            rows = pl.ds(pl.multiple_of(head * HEAD, HEAD), HEAD)
            for block in range(2):
                cols = slice(block * HALF, (block + 1) * HALF)
                keys = slice(0, (block + 1) * HALF)
                do_t = do_t_ref[0, rows, cols]
                q_t = q_t_ref[0, rows, cols]
                p_t = p_ref[0, head, keys, cols]
                row_sum = jnp.sum(
                    do_t.astype(F32) * o_t_ref[0, rows, cols].astype(F32), axis=0, keepdims=True
                )
                dp_t = mm(v_ref[group, keys, :], do_t)
                ds_t = (p_t.astype(F32) * (dp_t - row_sum)).astype(BF16)
                dq_ref[rows, cols] = mm(k_t_ref[0, kv_rows, keys], ds_t) * 0.125
                dk_new = mm(q_t, ds_t, NT)
                dv_new = mm(do_t, p_t, NT)
                for part in range(block + 1):
                    at = slice(part * HALF, (part + 1) * HALF)
                    dk[part] += dk_new[:, at]
                    dv[part] += dv_new[:, at]
        dq_ref[pl.ds(pl.multiple_of(D + group * HEAD, HEAD), HEAD), :] = jnp.concatenate(dk, axis=1)
        dqkv_ref[pl.ds(pl.multiple_of(D + KVW + group * HEAD, HEAD), HEAD), :] = jnp.concatenate(
            dv, axis=1
        ).astype(BF16)
        return carry

    lax.fori_loop(0, KV_HEADS, group_step, 0)
    dqkv_ref[: D + KVW] = rope_rows(
        dq_ref[...], cos_ref[0], sin_ref[0], HEADS + KV_HEADS, -1
    ).astype(BF16)


def attn_bwd(seq, args, handed):
    handed = list(handed)
    count = len(handed)
    hbm = pl.BlockSpec(memory_space=pl.ANY)
    return pl.pallas_call(
        functools.partial(attn_bwd_kernel, count),
        grid=(1,),
        in_specs=[
            seq_spec((32, SEQ), seq),
            seq_spec((32, SEQ), seq),
            seq_spec((D, SEQ), seq),
            seq_spec((KVW, SEQ), seq),
            seq_spec((KVW, SEQ), seq),
            seq_spec((HEADS, SEQ, SEQ), seq),
            seq_spec((D, SEQ), seq),
            seq_spec((D, SEQ), seq),
        ]
        + [hbm] * count,
        out_specs=[whole_spec((QKV, SEQ))] + [hbm] * count,
        out_shape=[jax.ShapeDtypeStruct((QKV, SEQ), BF16)]
        + [jax.ShapeDtypeStruct(v.shape, v.dtype) for v in handed],
        input_output_aliases={len(args) + k: 1 + k for k in range(count)},
        scratch_shapes=[
            pltpu.VMEM((D + KVW, SEQ), F32),
            pltpu.VMEM((KV_HEADS, SEQ, HEAD), BF16),
        ],
        compiler_params=pltpu.CompilerParams(vmem_limit_bytes=63 * 2**20),
        cost_estimate=pl.CostEstimate(flops=8 * 10**9, bytes_accessed=8 * 10**6, transcendentals=0),
        name="attn_bwd",
    )(*args, *handed)


def qkv_bwd_kernel(
    handed, where_ref, w_ref, gain_ref, dgain_two_ref, x_ref, h_t_ref, dx1_ref, dqkv0_ref, dqkv1_ref, *rest
):
    gx_ref, send_ref, keep_ref = rest[handed : handed + 3]
    dw_ref, dgain_ref, qs_ref, ks_ref, vs_ref, gs_ref, stage_ref = rest[-7:]
    dw = jnp.zeros((D, QKV), F32)
    dgain = jnp.zeros((D, 1), F32)
    for seq, dqkv_ref in enumerate((dqkv0_ref, dqkv1_ref)):
        dqkv = dqkv_ref[...]
        dh = mm(w_ref[...], dqkv)
        dw += mm(h_t_ref[seq], dqkv, NT)
        x = x_ref[seq].astype(F32)
        inv = lax.rsqrt(jnp.mean(x * x, axis=0, keepdims=True) + EPSILON)
        normed = x * inv
        dn = dh * gain_ref[:D]
        gx_ref[seq] = dx1_ref[seq] + inv * (
            dn - normed * jnp.mean(dn * normed, axis=0, keepdims=True)
        )
        dgain += jnp.sum(dh * normed, axis=1, keepdims=True)
    dw_ref[...] = dw
    dgain_ref[:D] = dgain
    dgain_ref[D:] = dgain_two_ref[...]
    join_square(qs_ref, dw_ref)
    for half in range(2):
        at = D + 96 * half
        ks_ref[pl.ds(half, D, stride=2), :96] = dw_ref[:, at : at + 96]
        vs_ref[pl.ds(half, D, stride=2), :96] = dw_ref[:, at + KVW : at + KVW + 96]
    for lane in range(9):
        gs_ref[:, lane : lane + 1] = dgain_ref[pl.ds(lane, 2 * CHIPS, stride=9), :]
    core = where_ref[0]
    stage_ref[...] = jnp.zeros_like(stage_ref)

    def spread(slot, carry):
        chip = chip_of(slot, where_ref, False)
        for keep_it in range(2):
            dev = chip * 2 + (core if keep_it else 1 - core)
            stage_ref[Q_QUERY : Q_QUERY + R_OUT, :] = get_rows(qs_ref, dev, R_OUT)
            stage_ref[Q_KEY : Q_KEY + R_KEY, :] = get_rows(ks_ref, dev, R_KEY)
            stage_ref[Q_VALUE : Q_VALUE + R_KEY, :] = get_rows(vs_ref, dev, R_KEY)
            stage_ref[Q_GAIN : Q_GAIN + 1, :] = get_rows(gs_ref, dev, 1)
            (keep_ref if keep_it else send_ref)[slot] = stage_ref[...].astype(BF16)
        return carry

    lax.fori_loop(0, CHIPS, spread, 0)


def qkv_bwd(args, handed):
    handed = list(handed)
    count = len(handed)
    hbm = pl.BlockSpec(memory_space=pl.ANY)
    seqs = args[4].shape[0]
    vmem = pl.BlockSpec(memory_space=pltpu.VMEM)
    return pl.pallas_call(
        functools.partial(qkv_bwd_kernel, count),
        in_specs=[pl.BlockSpec(memory_space=pltpu.SMEM)]
        + [vmem] * (len(args) - 1)
        + [hbm] * count,
        out_specs=[vmem] * 3 + [hbm] * count,
        out_shape=[
            jax.ShapeDtypeStruct((seqs, D, SEQ), F32),
            jax.ShapeDtypeStruct((CHIPS, ROWS_Q, 128), BF16),
            jax.ShapeDtypeStruct((CHIPS, ROWS_Q, 128), BF16),
        ]
        + [jax.ShapeDtypeStruct(v.shape, v.dtype) for v in handed],
        input_output_aliases={len(args) + k: 3 + k for k in range(count)},
        scratch_shapes=[
            pltpu.VMEM((D, QKV), F32),
            pltpu.VMEM((2 * D, 1), F32),
            pltpu.VMEM((2 * CHIPS * R_OUT, 128), F32),
            pltpu.VMEM((2 * CHIPS * R_KEY, 128), F32),
            pltpu.VMEM((2 * CHIPS * R_KEY, 128), F32),
            pltpu.VMEM((2 * CHIPS, 128), F32),
            pltpu.VMEM((ROWS_Q, 128), F32),
        ],
        compiler_params=pltpu.CompilerParams(vmem_limit_bytes=63 * 2**20),
        cost_estimate=pl.CostEstimate(flops=8 * 10**9, bytes_accessed=12 * 10**6, transcendentals=0),
        name="qkv_bwd",
    )(*args, *handed)


def pairs(axis, step):
    out = []
    for x in range(4):
        for y in range(4):
            for z in range(4):
                for core in range(2):
                    to = {"x": x, "y": y, "z": z, "c": core}
                    to[axis] = (to[axis] + step) % (2 if axis == "c" else 4)
                    me = ((x * 4 + y) * 4 + z) * 2 + core
                    out.append((me, ((to["x"] * 4 + to["y"]) * 4 + to["z"]) * 2 + to["c"]))
    return out


def hop(v, axis, step):
    return lax.ppermute(v, "dp", pairs(axis, step))


def sum_near(v, axis):
    low = v[1:].astype(BF16)
    got = [hop(low[k - 1], axis, k) for k in (2, 1, 3)]
    total = v[0].astype(F32)
    for piece in got:
        total = total + piece.astype(F32)
    return total


def ring_far(far, axis):
    cut = far.shape[0] // 2
    return hop(far[:cut], axis, 1).astype(F32), hop(far[cut:], axis, 3).astype(F32)


def ring_near(near, got, axis):
    cut = near.shape[1] // 2
    ahead = jnp.concatenate([near[0][:cut] + got[0], near[0][cut:]]).astype(BF16)
    behind = jnp.concatenate([near[1][:cut], near[1][cut:] + got[1]]).astype(BF16)
    return hop(ahead, axis, 1).astype(F32) + hop(behind, axis, 3).astype(F32)


def on_device(
    tokens, positions, norm_gains, w_query, w_key, w_value, w_out, w_gate, w_up, w_down, cotangent
):
    me = lax.axis_index("dp").astype(jnp.int32)
    where = jnp.stack([me % 2, me // 32, (me // 8) % 4, (me // 2) % 4])
    seqs = tokens.shape[0]
    x_t = jnp.swapaxes(tokens, 1, 2)
    cot_t = jnp.swapaxes(cotangent, 1, 2)

    pack_f, pack_q = pack(
        [
            lane_rows(jnp.concatenate([w_query, w_out]), 18, 288),
            jnp.concatenate([w_key, w_value]).reshape(18, 96),
            norm_gains.reshape(1, 9),
            lane_rows(w_down, 12, D),
            jnp.concatenate([w_gate, w_up]).reshape(2 * R_GATE, 128),
        ]
    )
    all_f = lax.all_gather(pack_f, "dp", axis=0, tiled=False)
    all_q = lax.all_to_all(
        jnp.broadcast_to(pack_q[None], (2 * CHIPS, ROWS_Q, 128)), "dp", split_axis=0, concat_axis=0
    )

    freqs = 100000.0 ** (-(jnp.arange(HEAD // 2, dtype=F32) * 2.0 / HEAD))
    angles = positions.astype(F32)[:, None, :] * freqs[None, :, None]
    cos_t = jnp.cos(angles)
    sin_t = jnp.sin(angles)
    fresh = (positions[:, 1:] != positions[:, :-1] + 1).astype(jnp.int32)
    docs = jnp.cumsum(jnp.pad(fresh, ((0, 0), (1, 0))), axis=1)

    wqkv, gain, h_t, q_t, k_t, v_t, p, o_t = attn_fwd(
        all_q, x_t, cos_t, sin_t, docs[:, None, :], docs[:, :, None]
    )
    y_t, dx1, do_t, dgain_two, send_g, keep_g, send_b, keep_b = ffn(
        where, all_f, x_t, o_t, cot_t, gain
    )
    got_g = hop(send_g, "c", 1)
    got_b = hop(send_b, "c", 1)
    args = [cos_t, sin_t, q_t, k_t, v_t, p, o_t, do_t]
    dqkv0, keep_g, keep_b = attn_bwd(0, args, [keep_g, keep_b])

    def halves(keep, got, rows):
        v = (keep.astype(F32) + got.astype(F32)).reshape(4, 4, 4, rows, 128)
        return v[2].astype(BF16), jnp.stack([v[1], v[3]]), v[0]

    far_g, near_g, own_g = halves(keep_g, got_g, ROWS_G)
    far_b, near_b, own_b = halves(keep_b, got_b, ROWS_B)
    got_g = ring_far(far_g, "z")
    got_b = ring_far(far_b, "y")
    dqkv1, near_g, near_b = attn_bwd(1, args, [near_g, near_b])
    sum_g = ring_near(near_g, got_g, "z")
    sum_b = ring_near(near_b, got_b, "y")
    gx_t, send_q, keep_q, own_g, own_b = qkv_bwd(
        [where, wqkv, gain, dgain_two, x_t, h_t, dx1, dqkv0, dqkv1], [own_g, own_b]
    )
    got_q = hop(send_q, "c", 1)
    sum_g = sum_g + own_g
    sum_b = sum_b + own_b
    sum_q = (keep_q.astype(F32) + got_q.astype(F32)).reshape(4, 4, 4, ROWS_Q, 128)
    sum_q = sum_near(sum_q, "z")
    sum_b = sum_near(sum_b, "z")
    sum_a = sum_near(jnp.concatenate([sum_g, sum_q], axis=2), "y")
    final = sum_near(jnp.concatenate([sum_a, sum_b], axis=1), "x")
    fg = final[:ROWS_G]
    fq = final[ROWS_G : ROWS_G + ROWS_Q]
    fb = final[ROWS_G + ROWS_Q :]
    return (
        jnp.swapaxes(y_t, 1, 2),
        jnp.swapaxes(gx_t, 1, 2),
        take_lanes(fq[Q_GAIN : Q_GAIN + 1], 1, 9),
        take_lanes(fq[Q_QUERY : Q_QUERY + R_OUT], 9, 288),
        take_lanes(fq[Q_KEY : Q_KEY + R_KEY], 9, 96),
        take_lanes(fq[Q_VALUE : Q_VALUE + R_KEY], 9, 96),
        take_lanes(fg[G_OUT : G_OUT + R_OUT], 9, 288),
        fb[B_GATE : B_GATE + R_GATE].reshape(-1),
        fb[B_UP : B_UP + R_GATE].reshape(-1),
        take_lanes(fg[G_DOWN : G_DOWN + R_DOWN], 12, D),
    )


def solution(mesh):
    flat = P("dp")
    cube = P("dp", None, None)
    return jax.shard_map(
        on_device,
        mesh=mesh,
        in_specs=(cube, P("dp", None)) + (flat,) * 8 + (cube,),
        out_specs=(cube, cube) + (flat,) * 8,
        check_vma=False,
    )
```

```python
import jax
import jax.numpy as jnp
from jax import lax
from jax.sharding import PartitionSpec as P
from jax.experimental import pallas as pl
from jax.experimental.pallas import tpu as pltpu

D = 576
HEADS = 9
KV_HEADS = 3
HEAD = 64
FF = 1536
SEQ = 512
KVW = KV_HEADS * HEAD
QKV = D + 2 * KVW
HALF = SEQ // 2

EPSILON = 1e-05
NEG_FILL = -1e30

F32 = jnp.float32
BF16 = jnp.bfloat16

CHIPS = 64
R_GATE = 54
R_DOWN = 60
R_OUT = 27
R_KEY = 9
F_GATE, F_UP, F_DOWN, F_OUT, ROWS_F = 0, 54, 112, 172, 208
B_GATE, B_UP, ROWS_B = 0, 54, 112
G_DOWN, G_OUT, ROWS_G = 0, 60, 96
Q_QUERY, Q_KEY, Q_VALUE, Q_GAIN, ROWS_Q = 0, 27, 36, 45, 48

NN = (((1,), (0,)), ((), ()))
NT = (((1,), (1,)), ((), ()))
TN = (((0,), (0,)), ((), ()))


def mm(a, b, dims=NN):
    return lax.dot_general(a, b, dims, preferred_element_type=F32)


def whole_spec(shape):
    zeros = (0,) * len(shape)
    return pl.BlockSpec(shape, lambda i: zeros)


def seq_spec(shape, at=None):
    zeros = (0,) * len(shape)
    return pl.BlockSpec((1,) + shape, lambda i: (i if at is None else at,) + zeros)


def chip_of(slot, where_ref, swap):
    one, two, three = slot // 16, (slot // 4) % 4, slot % 4
    kz, ky = (two, one) if swap else (one, two)
    x = (where_ref[1] + three) % 4
    y = (where_ref[2] + ky) % 4
    z = (where_ref[3] + kz) % 4
    return (x * 4 + y) * 4 + z


def put_rows(ref, dev, rows, val):
    ref[pl.ds(dev * rows, rows), :] = val


def get_rows(ref, dev, rows):
    return ref[pl.ds(dev * rows, rows), :]


def split_square(ref):
    parts = []
    for half in range(2):
        for j in range(3):
            piece = ref[pl.ds(3 * half + j, D, stride=6), :]
            parts.append(piece if j < 2 else piece[:, :32])
    return parts


def join_square(ref, val_ref):
    for half in range(2):
        for j in range(3):
            width = 128 if j < 2 else 32
            at = 288 * half + 128 * j
            ref[pl.ds(3 * half + j, D, stride=6), :width] = val_ref[:, at : at + width]


def pack_kernel(wqo, wkv, gn, wd, wgu, f_ref, q_ref, f_stage_ref, q_stage_ref):
    f_stage_ref[...] = jnp.zeros_like(f_stage_ref)
    q_stage_ref[...] = jnp.zeros_like(q_stage_ref)
    square = wqo[...].astype(F32)
    thin = wkv[...].astype(F32)
    for ref, at, val in (
        (q_stage_ref, Q_QUERY, square[:R_OUT]),
        (q_stage_ref, Q_KEY, thin[:R_KEY]),
        (q_stage_ref, Q_VALUE, thin[R_KEY:]),
        (q_stage_ref, Q_GAIN, gn[...].astype(F32)),
        (f_stage_ref, F_GATE, wgu[...].astype(F32)),
        (f_stage_ref, F_DOWN, wd[...].astype(F32)),
        (f_stage_ref, F_OUT, square[R_OUT:]),
    ):
        ref[at : at + val.shape[0], : val.shape[1]] = val
    f_ref[...] = f_stage_ref[...].astype(BF16)
    q_ref[...] = q_stage_ref[...].astype(BF16)


def pack(pieces):
    vmem = pl.BlockSpec(memory_space=pltpu.VMEM)
    return pl.pallas_call(
        pack_kernel,
        in_specs=[vmem] * 5,
        out_specs=[vmem] * 2,
        out_shape=[
            jax.ShapeDtypeStruct((ROWS_F, 128), BF16),
            jax.ShapeDtypeStruct((ROWS_Q, 128), BF16),
        ],
        scratch_shapes=[pltpu.VMEM((ROWS_F, 128), F32), pltpu.VMEM((ROWS_Q, 128), F32)],
        name="pack",
    )(*pieces)


def lane_rows(v, rows, width):
    v = v.reshape(rows, width)
    full = -(-width // 128) * 128
    v = jnp.pad(v, ((0, 0), (0, full - width)))
    return v.reshape(rows * full // 128, 128)


def take_lanes(v, rows, width):
    full = -(-width // 128) * 128
    return v.reshape(rows, full)[:, :width].reshape(-1)


def rope_rows(v, cos_t, sin_t, heads, sign):
    out = []
    for head in range(heads):
        lo = v[head * HEAD : head * HEAD + 32]
        hi = v[head * HEAD + 32 : head * HEAD + 64]
        if sign > 0:
            out += [lo * cos_t - hi * sin_t, hi * cos_t + lo * sin_t]
        else:
            out += [lo * cos_t + hi * sin_t, hi * cos_t - lo * sin_t]
    return jnp.concatenate(out, axis=0)


def attn_fwd_kernel(
    pack_ref, x_ref, cos_ref, sin_ref, docr_ref, docc_ref,
    wqkv_ref, gain_ref, h_t_ref, q_t_ref, k_t_ref, v_t_ref, p_ref, o_t_ref,
    qs_ref, ks_ref, vs_ref, gs_ref, w_t_ref, bias_ref, k_ref,
):
    @pl.when(pl.program_id(0) == 0)
    def _():
        def squeeze(dev, carry):
            val = pack_ref[dev].astype(F32)
            put_rows(qs_ref, dev, R_OUT, val[Q_QUERY : Q_QUERY + R_OUT])
            put_rows(ks_ref, dev, R_KEY, val[Q_KEY : Q_KEY + R_KEY])
            put_rows(vs_ref, dev, R_KEY, val[Q_VALUE : Q_VALUE + R_KEY])
            put_rows(gs_ref, dev, 1, val[Q_GAIN : Q_GAIN + 1])
            return carry

        lax.fori_loop(0, 2 * CHIPS, squeeze, 0)
        parts = split_square(qs_ref)
        for ref in (ks_ref, vs_ref):
            for half in range(2):
                parts.append(ref[pl.ds(half, D, stride=2), :][:, :96])
        whole = jnp.concatenate(parts, axis=1)
        wqkv_ref[...] = whole.astype(BF16)
        w_t_ref[...] = whole.T.astype(BF16)
        for lane in range(9):
            gain_ref[pl.ds(lane, 2 * CHIPS, stride=9), :] = gs_ref[:, lane : lane + 1]

    x = x_ref[0].astype(F32)
    inv = lax.rsqrt(jnp.mean(x * x, axis=0, keepdims=True) + EPSILON)
    h_t = ((x * inv) * gain_ref[:D]).astype(BF16)
    h_t_ref[0] = h_t
    cos_t = cos_ref[0]
    sin_t = sin_ref[0]
    q_t = mm(w_t_ref[:D], h_t)
    q_t_ref[0] = rope_rows(q_t, cos_t, sin_t, HEADS, 1).astype(BF16) * 0.125
    k_t = rope_rows(mm(w_t_ref[D : D + KVW], h_t), cos_t, sin_t, KV_HEADS, 1).astype(BF16)
    k_t_ref[0] = k_t
    for group in range(KV_HEADS):
        k_ref[group] = k_t[group * HEAD : (group + 1) * HEAD].astype(F32).T.astype(BF16)
    v_t_ref[0] = mm(w_t_ref[D + KVW :], h_t).astype(BF16)
    key_at = lax.broadcasted_iota(jnp.int32, (SEQ, SEQ), 0)
    query_at = lax.broadcasted_iota(jnp.int32, (SEQ, SEQ), 1)
    same = docc_ref[0] == docr_ref[0]
    bias_ref[...] = jnp.where(same & (key_at <= query_at), 0.0, NEG_FILL)

    def group_step(group, carry):
        kv_rows = pl.ds(pl.multiple_of(group * HEAD, HEAD), HEAD)
        for member in range(HEADS // KV_HEADS):
            head = group * (HEADS // KV_HEADS) + member
            rows = pl.ds(pl.multiple_of(head * HEAD, HEAD), HEAD)
            for block in range(2):
                cols = slice(block * HALF, (block + 1) * HALF)
                keys = slice(0, (block + 1) * HALF)
                s_t = mm(k_ref[group, keys, :], q_t_ref[0, rows, cols]) + bias_ref[keys, cols]
                peak = jnp.max(s_t, axis=0, keepdims=True)
                e_t = jnp.exp(s_t - peak)
                scale = 1.0 / jnp.sum(e_t, axis=0, keepdims=True)
                p_t = (e_t * scale).astype(BF16)
                p_ref[0, head, keys, cols] = p_t
                o_t_ref[0, rows, cols] = mm(v_t_ref[0, kv_rows, keys], p_t).astype(BF16)
        return carry

    lax.fori_loop(0, KV_HEADS, group_step, 0)


def attn_fwd(pack_q, x_t, cos_t, sin_t, doc_row, doc_col):
    seqs = x_t.shape[0]
    out = [
        ((D, QKV), BF16, False),
        ((2 * D, 1), F32, False),
        ((D, SEQ), BF16, True),
        ((D, SEQ), BF16, True),
        ((KVW, SEQ), BF16, True),
        ((KVW, SEQ), BF16, True),
        ((HEADS, SEQ, SEQ), BF16, True),
        ((D, SEQ), BF16, True),
    ]
    return pl.pallas_call(
        attn_fwd_kernel,
        grid=(seqs,),
        in_specs=[
            whole_spec((2 * CHIPS, ROWS_Q, 128)),
            seq_spec((D, SEQ)),
            seq_spec((32, SEQ)),
            seq_spec((32, SEQ)),
            seq_spec((1, SEQ)),
            seq_spec((SEQ, 1)),
        ],
        out_specs=[seq_spec(s) if per else whole_spec(s) for s, _, per in out],
        out_shape=[jax.ShapeDtypeStruct(((seqs,) + s) if per else s, t) for s, t, per in out],
        scratch_shapes=[
            pltpu.VMEM((2 * CHIPS * R_OUT, 128), F32),
            pltpu.VMEM((2 * CHIPS * R_KEY, 128), F32),
            pltpu.VMEM((2 * CHIPS * R_KEY, 128), F32),
            pltpu.VMEM((2 * CHIPS, 128), F32),
            pltpu.VMEM((QKV, D), BF16),
            pltpu.VMEM((SEQ, SEQ), F32),
            pltpu.VMEM((KV_HEADS, SEQ, HEAD), BF16),
        ],
        compiler_params=pltpu.CompilerParams(vmem_limit_bytes=63 * 2**20),
        cost_estimate=pl.CostEstimate(
            flops=8 * 10**9, bytes_accessed=20 * 10**6, transcendentals=5 * 10**6
        ),
        name="attn_fwd",
    )(pack_q, x_t, cos_t, sin_t, doc_row, doc_col)


CHUNK = 256
CHUNKS = FF // CHUNK


def ffn_kernel(
    where_ref, pack_ref, x_ref, o_t_ref, cot_ref, gain_ref,
    y_ref, dx1_ref, do_t_ref, dgain_ref, send_g_ref, keep_g_ref, send_b_ref, keep_b_ref,
    gs_ref, us_ref, ds_ref, os_ref, wg_ref, wu_ref, wd_ref, wo_ref,
    acc_ref, h_t_ref, gb_ref, dh_ref, inv_ref, stage_ref,
):
    seqs = x_ref.shape[0]
    core = where_ref[0]

    def squeeze(dev, carry):
        val = pack_ref[dev].astype(F32)
        put_rows(gs_ref, dev, R_GATE, val[F_GATE : F_GATE + R_GATE])
        put_rows(us_ref, dev, R_GATE, val[F_UP : F_UP + R_GATE])
        put_rows(ds_ref, dev, R_DOWN, val[F_DOWN : F_DOWN + R_DOWN])
        put_rows(os_ref, dev, R_OUT, val[F_OUT : F_OUT + R_OUT])
        return carry

    lax.fori_loop(0, 2 * CHIPS, squeeze, 0)
    wo_ref[...] = jnp.concatenate(split_square(os_ref), axis=1).astype(BF16)
    for j in range(12):
        cols = slice(j * 128, (j + 1) * 128)
        wg_ref[:, cols] = gs_ref[pl.ds(j, D, stride=12), :].astype(BF16)
        wu_ref[:, cols] = us_ref[pl.ds(j, D, stride=12), :].astype(BF16)
    for j in range(5):
        width = min(128, D - j * 128)
        wd_ref[:, j * 128 : j * 128 + width] = ds_ref[pl.ds(j, FF, stride=5), :][:, :width].astype(BF16)

    gain = gain_ref[D:]
    for seq in range(seqs):
        cols = slice(seq * SEQ, (seq + 1) * SEQ)
        x1 = x_ref[seq].astype(F32) + mm(wo_ref[...], o_t_ref[seq], TN)
        inv = lax.rsqrt(jnp.mean(x1 * x1, axis=0, keepdims=True) + EPSILON)
        normed = x1 * inv
        acc_ref[:, cols] = x1
        inv_ref[:, cols] = inv
        dx1_ref[seq] = normed
        h_t_ref[:, cols] = (normed * gain).astype(BF16)
        gb_ref[:, cols] = cot_ref[seq].astype(BF16)
    dh_ref[...] = jnp.zeros_like(dh_ref)

    def chunk_step(chunk, carry):
        cols = pl.ds(pl.multiple_of(chunk * CHUNK, CHUNK), CHUNK)
        wg = wg_ref[:, cols]
        wu = wu_ref[:, cols]
        wd = wd_ref[cols, :]
        h_t = h_t_ref[...]
        gb = gb_ref[...]
        a = mm(wg, h_t, TN)
        b = mm(wu, h_t, TN)
        dm = mm(wd, gb)
        sg = 1.0 / (1.0 + jnp.exp(-a))
        silu = a * sg
        m = (silu * b).astype(BF16)
        da = (dm * b * sg * (1.0 + a * (1.0 - sg))).astype(BF16)
        db = (dm * silu).astype(BF16)
        acc_ref[...] += mm(wd, m, TN)
        dh_ref[...] += mm(wg, da) + mm(wu, db)
        dwg = mm(h_t, da, NT)
        dwu = mm(h_t, db, NT)
        dwd = mm(m, gb, NT)
        for j in range(CHUNK // 128):
            lane = slice(j * 128, (j + 1) * 128)
            at = chunk * (CHUNK // 128) + j
            gs_ref[pl.ds(at, D, stride=12), :] = dwg[:, lane]
            us_ref[pl.ds(at, D, stride=12), :] = dwu[:, lane]
        for j in range(5):
            width = min(128, D - j * 128)
            ds_ref[pl.ds(chunk * CHUNK * 5 + j, CHUNK, stride=5), :width] = dwd[
                :, j * 128 : j * 128 + width
            ]
        return carry

    lax.fori_loop(0, CHUNKS, chunk_step, 0)

    dgain = jnp.zeros((D, 1), F32)
    dwo = jnp.zeros((D, D), F32)
    for seq in range(seqs):
        cols = slice(seq * SEQ, (seq + 1) * SEQ)
        y_ref[seq] = acc_ref[:, cols].astype(BF16)
        dh = dh_ref[:, cols]
        normed = dx1_ref[seq]
        dgain += jnp.sum(dh * normed, axis=1, keepdims=True)
        dn = dh * gain
        dx1 = cot_ref[seq] + inv_ref[:, cols] * (
            dn - normed * jnp.mean(dn * normed, axis=0, keepdims=True)
        )
        dx1_ref[seq] = dx1
        low = dx1.astype(BF16)
        dwo += mm(o_t_ref[seq], low, NT)
        do_t_ref[seq] = mm(wo_ref[...], low).astype(BF16)
    dgain_ref[...] = dgain
    dh_ref[:, :D] = dwo
    join_square(os_ref, dh_ref)

    stage_ref[...] = jnp.zeros_like(stage_ref)

    def spread(slot, carry):
        for keep_it in range(2):
            chip = chip_of(slot, where_ref, False)
            dev = chip * 2 + (core if keep_it else 1 - core)
            stage_ref[G_DOWN : G_DOWN + R_DOWN, :] = get_rows(ds_ref, dev, R_DOWN)
            stage_ref[G_OUT : G_OUT + R_OUT, :] = get_rows(os_ref, dev, R_OUT)
            (keep_g_ref if keep_it else send_g_ref)[slot] = stage_ref[:ROWS_G].astype(BF16)
            chip = chip_of(slot, where_ref, True)
            dev = chip * 2 + (core if keep_it else 1 - core)
            stage_ref[B_GATE : B_GATE + R_GATE, :] = get_rows(gs_ref, dev, R_GATE)
            stage_ref[B_UP : B_UP + R_GATE, :] = get_rows(us_ref, dev, R_GATE)
            (keep_b_ref if keep_it else send_b_ref)[slot] = stage_ref[...].astype(BF16)
        return carry

    lax.fori_loop(0, CHIPS, spread, 0)


def ffn(where, pack_f, x_t, o_t, cot_t, gain):
    seqs = x_t.shape[0]
    cols_all = seqs * SEQ
    vmem = pl.BlockSpec(memory_space=pltpu.VMEM)
    return pl.pallas_call(
        ffn_kernel,
        in_specs=[pl.BlockSpec(memory_space=pltpu.SMEM)] + [vmem] * 5,
        out_specs=[vmem] * 8,
        out_shape=[
            jax.ShapeDtypeStruct((seqs, D, SEQ), BF16),
            jax.ShapeDtypeStruct((seqs, D, SEQ), F32),
            jax.ShapeDtypeStruct((seqs, D, SEQ), BF16),
            jax.ShapeDtypeStruct((D, 1), F32),
            jax.ShapeDtypeStruct((CHIPS, ROWS_G, 128), BF16),
            jax.ShapeDtypeStruct((CHIPS, ROWS_G, 128), BF16),
            jax.ShapeDtypeStruct((CHIPS, ROWS_B, 128), BF16),
            jax.ShapeDtypeStruct((CHIPS, ROWS_B, 128), BF16),
        ],
        scratch_shapes=[
            pltpu.VMEM((2 * CHIPS * R_GATE, 128), F32),
            pltpu.VMEM((2 * CHIPS * R_GATE, 128), F32),
            pltpu.VMEM((2 * CHIPS * R_DOWN, 128), F32),
            pltpu.VMEM((2 * CHIPS * R_OUT, 128), F32),
            pltpu.VMEM((D, FF), BF16),
            pltpu.VMEM((D, FF), BF16),
            pltpu.VMEM((FF, D), BF16),
            pltpu.VMEM((D, D), BF16),
            pltpu.VMEM((D, cols_all), F32),
            pltpu.VMEM((D, cols_all), BF16),
            pltpu.VMEM((D, cols_all), BF16),
            pltpu.VMEM((D, cols_all), F32),
            pltpu.VMEM((1, cols_all), F32),
            pltpu.VMEM((ROWS_B, 128), F32),
        ],
        compiler_params=pltpu.CompilerParams(vmem_limit_bytes=63 * 2**20),
        cost_estimate=pl.CostEstimate(
            flops=25 * 10**9, bytes_accessed=30 * 10**6, transcendentals=2 * 10**6
        ),
        name="ffn",
    )(where, pack_f, x_t, o_t, cot_t, gain)


def attn_bwd_kernel(
    cos_ref, sin_ref, q_t_ref, k_t_ref, v_t_ref, p_ref, o_t_ref, do_t_ref, *rest
):
    dqkv_ref, zero_ref, dq_ref, v_ref = rest[-4:]
    zero_ref[...] = jnp.zeros_like(zero_ref)
    for group in range(KV_HEADS):
        v_ref[group] = v_t_ref[0, group * HEAD : (group + 1) * HEAD, :].astype(F32).T.astype(BF16)

    def group_step(group, carry):
        kv_rows = pl.ds(pl.multiple_of(group * HEAD, HEAD), HEAD)
        dk = [jnp.zeros((HEAD, HALF), F32) for _ in range(2)]
        dv = [jnp.zeros((HEAD, HALF), F32) for _ in range(2)]
        for member in range(HEADS // KV_HEADS):
            head = group * (HEADS // KV_HEADS) + member
            rows = pl.ds(pl.multiple_of(head * HEAD, HEAD), HEAD)
            for block in range(2):
                cols = slice(block * HALF, (block + 1) * HALF)
                keys = slice(0, (block + 1) * HALF)
                do_t = do_t_ref[0, rows, cols]
                q_t = q_t_ref[0, rows, cols]
                p_t = p_ref[0, head, keys, cols]
                row_sum = jnp.sum(
                    do_t.astype(F32) * o_t_ref[0, rows, cols].astype(F32), axis=0, keepdims=True
                )
                dp_t = mm(v_ref[group, keys, :], do_t)
                ds_t = (p_t.astype(F32) * (dp_t - row_sum)).astype(BF16)
                dq_ref[rows, cols] = mm(k_t_ref[0, kv_rows, keys], ds_t) * 0.125
                dk_new = mm(q_t, ds_t, NT)
                dv_new = mm(do_t, p_t, NT)
                for part in range(block + 1):
                    at = slice(part * HALF, (part + 1) * HALF)
                    dk[part] += dk_new[:, at]
                    dv[part] += dv_new[:, at]
        dq_ref[pl.ds(pl.multiple_of(D + group * HEAD, HEAD), HEAD), :] = jnp.concatenate(dk, axis=1)
        dqkv_ref[pl.ds(pl.multiple_of(D + KVW + group * HEAD, HEAD), HEAD), :] = jnp.concatenate(
            dv, axis=1
        ).astype(BF16)
        return carry

    lax.fori_loop(0, KV_HEADS, group_step, 0)
    dqkv_ref[: D + KVW] = rope_rows(
        dq_ref[...], cos_ref[0], sin_ref[0], HEADS + KV_HEADS, -1
    ).astype(BF16)


def attn_bwd(seq, args, after):
    return pl.pallas_call(
        attn_bwd_kernel,
        grid=(1,),
        in_specs=[
            seq_spec((32, SEQ), seq),
            seq_spec((32, SEQ), seq),
            seq_spec((D, SEQ), seq),
            seq_spec((KVW, SEQ), seq),
            seq_spec((KVW, SEQ), seq),
            seq_spec((HEADS, SEQ, SEQ), seq),
            seq_spec((D, SEQ), seq),
            seq_spec((D, SEQ), seq),
        ]
        + [pl.BlockSpec(memory_space=pl.ANY)] * len(after),
        out_specs=[whole_spec((QKV, SEQ)), whole_spec((8, 128))],
        out_shape=[
            jax.ShapeDtypeStruct((QKV, SEQ), BF16),
            jax.ShapeDtypeStruct((8, 128), F32),
        ],
        scratch_shapes=[
            pltpu.VMEM((D + KVW, SEQ), F32),
            pltpu.VMEM((KV_HEADS, SEQ, HEAD), BF16),
        ],
        compiler_params=pltpu.CompilerParams(vmem_limit_bytes=63 * 2**20),
        cost_estimate=pl.CostEstimate(flops=8 * 10**9, bytes_accessed=8 * 10**6, transcendentals=0),
        name="attn_bwd",
    )(*args, *after)


def qkv_bwd_kernel(
    where_ref, w_ref, gain_ref, dgain_two_ref, x_ref, h_t_ref, dx1_ref, dqkv0_ref, dqkv1_ref, *rest
):
    gx_ref, send_ref, keep_ref, zero_ref = rest[-11:-7]
    dw_ref, dgain_ref, qs_ref, ks_ref, vs_ref, gs_ref, stage_ref = rest[-7:]
    zero_ref[...] = jnp.zeros_like(zero_ref)
    dw = jnp.zeros((D, QKV), F32)
    dgain = jnp.zeros((D, 1), F32)
    for seq, dqkv_ref in enumerate((dqkv0_ref, dqkv1_ref)):
        dqkv = dqkv_ref[...]
        dh = mm(w_ref[...], dqkv)
        dw += mm(h_t_ref[seq], dqkv, NT)
        x = x_ref[seq].astype(F32)
        inv = lax.rsqrt(jnp.mean(x * x, axis=0, keepdims=True) + EPSILON)
        normed = x * inv
        dn = dh * gain_ref[:D]
        gx_ref[seq] = dx1_ref[seq] + inv * (
            dn - normed * jnp.mean(dn * normed, axis=0, keepdims=True)
        )
        dgain += jnp.sum(dh * normed, axis=1, keepdims=True)
    dw_ref[...] = dw
    dgain_ref[:D] = dgain
    dgain_ref[D:] = dgain_two_ref[...]
    join_square(qs_ref, dw_ref)
    for half in range(2):
        at = D + 96 * half
        ks_ref[pl.ds(half, D, stride=2), :96] = dw_ref[:, at : at + 96]
        vs_ref[pl.ds(half, D, stride=2), :96] = dw_ref[:, at + KVW : at + KVW + 96]
    for lane in range(9):
        gs_ref[:, lane : lane + 1] = dgain_ref[pl.ds(lane, 2 * CHIPS, stride=9), :]
    core = where_ref[0]
    stage_ref[...] = jnp.zeros_like(stage_ref)

    def spread(slot, carry):
        chip = chip_of(slot, where_ref, False)
        for keep_it in range(2):
            dev = chip * 2 + (core if keep_it else 1 - core)
            stage_ref[Q_QUERY : Q_QUERY + R_OUT, :] = get_rows(qs_ref, dev, R_OUT)
            stage_ref[Q_KEY : Q_KEY + R_KEY, :] = get_rows(ks_ref, dev, R_KEY)
            stage_ref[Q_VALUE : Q_VALUE + R_KEY, :] = get_rows(vs_ref, dev, R_KEY)
            stage_ref[Q_GAIN : Q_GAIN + 1, :] = get_rows(gs_ref, dev, 1)
            (keep_ref if keep_it else send_ref)[slot] = stage_ref[...].astype(BF16)
        return carry

    lax.fori_loop(0, CHIPS, spread, 0)


def qkv_bwd(args, after):
    seqs = args[4].shape[0]
    vmem = pl.BlockSpec(memory_space=pltpu.VMEM)
    return pl.pallas_call(
        qkv_bwd_kernel,
        in_specs=[pl.BlockSpec(memory_space=pltpu.SMEM)]
        + [vmem] * (len(args) - 1)
        + [pl.BlockSpec(memory_space=pl.ANY)] * len(after),
        out_specs=[vmem] * 4,
        out_shape=[
            jax.ShapeDtypeStruct((seqs, D, SEQ), F32),
            jax.ShapeDtypeStruct((CHIPS, ROWS_Q, 128), BF16),
            jax.ShapeDtypeStruct((CHIPS, ROWS_Q, 128), BF16),
            jax.ShapeDtypeStruct((8, 128), F32),
        ],
        scratch_shapes=[
            pltpu.VMEM((D, QKV), F32),
            pltpu.VMEM((2 * D, 1), F32),
            pltpu.VMEM((2 * CHIPS * R_OUT, 128), F32),
            pltpu.VMEM((2 * CHIPS * R_KEY, 128), F32),
            pltpu.VMEM((2 * CHIPS * R_KEY, 128), F32),
            pltpu.VMEM((2 * CHIPS, 128), F32),
            pltpu.VMEM((ROWS_Q, 128), F32),
        ],
        compiler_params=pltpu.CompilerParams(vmem_limit_bytes=63 * 2**20),
        cost_estimate=pl.CostEstimate(flops=8 * 10**9, bytes_accessed=12 * 10**6, transcendentals=0),
        name="qkv_bwd",
    )(*args, *after)


def pairs(axis, step):
    out = []
    for x in range(4):
        for y in range(4):
            for z in range(4):
                for core in range(2):
                    to = {"x": x, "y": y, "z": z, "c": core}
                    to[axis] = (to[axis] + step) % (2 if axis == "c" else 4)
                    me = ((x * 4 + y) * 4 + z) * 2 + core
                    out.append((me, ((to["x"] * 4 + to["y"]) * 4 + to["z"]) * 2 + to["c"]))
    return out


def hop(v, axis, step):
    return lax.ppermute(v, "dp", pairs(axis, step))


def sum_near(v, axis):
    low = v[1:].astype(BF16)
    got = [hop(low[k - 1], axis, k) for k in (2, 1, 3)]
    total = v[0].astype(F32)
    for piece in got:
        total = total + piece.astype(F32)
    return total


def both(keep, got, place, zero):
    rows = keep.shape[1]
    keep = keep.reshape(4, 4, 4, rows, 128)[place]
    got = got.reshape(4, 4, 4, rows, 128)[place]
    return keep.astype(F32) + got.astype(F32) + zero[0, 0]


def ring_far(far, axis):
    return hop(far[:2], axis, 1).astype(F32), hop(far[2:], axis, 3).astype(F32)


def ring_near(keep, got, arrived, zero):
    ahead, behind = both(keep, got, 1, zero), both(keep, got, 3, zero)
    ahead = jnp.concatenate([ahead[:2] + arrived[0], ahead[2:]])
    behind = jnp.concatenate([behind[:2], behind[2:] + arrived[1]])
    return ahead.astype(BF16), behind.astype(BF16)


def on_device(
    tokens, positions, norm_gains, w_query, w_key, w_value, w_out, w_gate, w_up, w_down, cotangent
):
    me = lax.axis_index("dp").astype(jnp.int32)
    where = jnp.stack([me % 2, me // 32, (me // 8) % 4, (me // 2) % 4])
    seqs = tokens.shape[0]
    x_t = jnp.swapaxes(tokens, 1, 2)
    cot_t = jnp.swapaxes(cotangent, 1, 2)

    pack_f, pack_q = pack(
        [
            lane_rows(jnp.concatenate([w_query, w_out]), 18, 288),
            jnp.concatenate([w_key, w_value]).reshape(18, 96),
            norm_gains.reshape(1, 9),
            lane_rows(w_down, 12, D),
            jnp.concatenate([w_gate, w_up]).reshape(2 * R_GATE, 128),
        ]
    )
    all_f = lax.all_gather(pack_f, "dp", axis=0, tiled=False)
    all_q = lax.all_to_all(
        jnp.broadcast_to(pack_q[None], (2 * CHIPS, ROWS_Q, 128)), "dp", split_axis=0, concat_axis=0
    )

    freqs = 100000.0 ** (-(jnp.arange(HEAD // 2, dtype=F32) * 2.0 / HEAD))
    angles = positions.astype(F32)[:, None, :] * freqs[None, :, None]
    cos_t = jnp.cos(angles)
    sin_t = jnp.sin(angles)
    fresh = (positions[:, 1:] != positions[:, :-1] + 1).astype(jnp.int32)
    docs = jnp.cumsum(jnp.pad(fresh, ((0, 0), (1, 0))), axis=1)

    wqkv, gain, h_t, q_t, k_t, v_t, p, o_t = attn_fwd(
        all_q, x_t, cos_t, sin_t, docs[:, None, :], docs[:, :, None]
    )
    y_t, dx1, do_t, dgain_two, send_g, keep_g, send_b, keep_b = ffn(
        where, all_f, x_t, o_t, cot_t, gain
    )
    got_g = hop(send_g, "c", 1)
    got_b = hop(send_b, "c", 1)
    args = [cos_t, sin_t, q_t, k_t, v_t, p, o_t, do_t]
    dqkv0, zero = attn_bwd(0, args, [])
    far_g = both(keep_g, got_g, 2, zero).astype(BF16)
    far_b = both(keep_b, got_b, 2, zero).astype(BF16)
    dqkv1, zero = attn_bwd(1, args, [far_g, far_b])
    near_g = ring_near(keep_g, got_g, ring_far(far_g, "z"), zero)
    near_b = ring_near(keep_b, got_b, ring_far(far_b, "y"), zero)
    gx_t, send_q, keep_q, zero = qkv_bwd(
        [where, wqkv, gain, dgain_two, x_t, h_t, dx1, dqkv0, dqkv1], near_g + near_b
    )
    got_q = hop(send_q, "c", 1)
    sum_g = both(keep_g, got_g, 0, zero)
    sum_g = sum_g + hop(near_g[0], "z", 1).astype(F32) + hop(near_g[1], "z", 3).astype(F32)
    sum_b = both(keep_b, got_b, 0, zero)
    sum_b = sum_b + hop(near_b[0], "y", 1).astype(F32) + hop(near_b[1], "y", 3).astype(F32)
    sum_q = (keep_q.astype(F32) + got_q.astype(F32)).reshape(4, 4, 4, ROWS_Q, 128)
    sum_q = sum_near(sum_q, "z")
    sum_b = sum_near(sum_b, "z")
    sum_a = sum_near(jnp.concatenate([sum_g, sum_q], axis=2), "y")
    final = sum_near(jnp.concatenate([sum_a, sum_b], axis=1), "x")
    fg = final[:ROWS_G]
    fq = final[ROWS_G : ROWS_G + ROWS_Q]
    fb = final[ROWS_G + ROWS_Q :]
    return (
        jnp.swapaxes(y_t, 1, 2),
        jnp.swapaxes(gx_t, 1, 2),
        take_lanes(fq[Q_GAIN : Q_GAIN + 1], 1, 9),
        take_lanes(fq[Q_QUERY : Q_QUERY + R_OUT], 9, 288),
        take_lanes(fq[Q_KEY : Q_KEY + R_KEY], 9, 96),
        take_lanes(fq[Q_VALUE : Q_VALUE + R_KEY], 9, 96),
        take_lanes(fg[G_OUT : G_OUT + R_OUT], 9, 288),
        fb[B_GATE : B_GATE + R_GATE].reshape(-1),
        fb[B_UP : B_UP + R_GATE].reshape(-1),
        take_lanes(fg[G_DOWN : G_DOWN + R_DOWN], 12, D),
    )


def solution(mesh):
    flat = P("dp")
    cube = P("dp", None, None)
    return jax.shard_map(
        on_device,
        mesh=mesh,
        in_specs=(cube, P("dp", None)) + (flat,) * 8 + (cube,),
        out_specs=(cube, cube) + (flat,) * 8,
        check_vma=False,
    )
```

```python
import jax
import jax.numpy as jnp
from jax import lax
from jax.sharding import PartitionSpec as P
from jax.experimental import pallas as pl
from jax.experimental.pallas import tpu as pltpu

D = 576
HEADS = 9
KV_HEADS = 3
HEAD = 64
FF = 1536
SEQ = 512
KVW = KV_HEADS * HEAD
QKV = D + 2 * KVW
HALF = SEQ // 2

EPSILON = 1e-05
NEG_FILL = -1e30

F32 = jnp.float32
BF16 = jnp.bfloat16

CHIPS = 64
R_GATE = 54
R_DOWN = 60
R_OUT = 27
R_KEY = 9
F_GATE, F_UP, F_DOWN, F_OUT, ROWS_F = 0, 54, 112, 172, 208
B_GATE, B_UP, ROWS_B = 0, 54, 112
G_DOWN, G_OUT, ROWS_G = 0, 60, 96
Q_QUERY, Q_KEY, Q_VALUE, Q_GAIN, ROWS_Q = 0, 27, 36, 45, 48

NN = (((1,), (0,)), ((), ()))
NT = (((1,), (1,)), ((), ()))
TN = (((0,), (0,)), ((), ()))


def mm(a, b, dims=NN):
    return lax.dot_general(a, b, dims, preferred_element_type=F32)


def whole_spec(shape):
    zeros = (0,) * len(shape)
    return pl.BlockSpec(shape, lambda i: zeros)


def seq_spec(shape, at=None):
    zeros = (0,) * len(shape)
    return pl.BlockSpec((1,) + shape, lambda i: (i if at is None else at,) + zeros)


def chip_of(slot, where_ref, swap):
    one, two, three = slot // 16, (slot // 4) % 4, slot % 4
    kz, ky = (two, one) if swap else (one, two)
    x = (where_ref[1] + three) % 4
    y = (where_ref[2] + ky) % 4
    z = (where_ref[3] + kz) % 4
    return (x * 4 + y) * 4 + z


def put_rows(ref, dev, rows, val):
    ref[pl.ds(dev * rows, rows), :] = val


def get_rows(ref, dev, rows):
    return ref[pl.ds(dev * rows, rows), :]


def split_square(ref):
    parts = []
    for half in range(2):
        for j in range(3):
            piece = ref[pl.ds(3 * half + j, D, stride=6), :]
            parts.append(piece if j < 2 else piece[:, :32])
    return parts


def join_square(ref, val_ref):
    for half in range(2):
        for j in range(3):
            width = 128 if j < 2 else 32
            at = 288 * half + 128 * j
            ref[pl.ds(3 * half + j, D, stride=6), :width] = val_ref[:, at : at + width]


def pack_kernel(wqo, wkv, gn, wd, wgu, f_ref, q_ref, f_stage_ref, q_stage_ref):
    f_stage_ref[...] = jnp.zeros_like(f_stage_ref)
    q_stage_ref[...] = jnp.zeros_like(q_stage_ref)
    square = wqo[...].astype(F32)
    thin = wkv[...].astype(F32)
    for ref, at, val in (
        (q_stage_ref, Q_QUERY, square[:R_OUT]),
        (q_stage_ref, Q_KEY, thin[:R_KEY]),
        (q_stage_ref, Q_VALUE, thin[R_KEY:]),
        (q_stage_ref, Q_GAIN, gn[...].astype(F32)),
        (f_stage_ref, F_GATE, wgu[...].astype(F32)),
        (f_stage_ref, F_DOWN, wd[...].astype(F32)),
        (f_stage_ref, F_OUT, square[R_OUT:]),
    ):
        ref[at : at + val.shape[0], : val.shape[1]] = val
    f_ref[...] = f_stage_ref[...].astype(BF16)
    q_ref[...] = q_stage_ref[...].astype(BF16)


def pack(pieces):
    vmem = pl.BlockSpec(memory_space=pltpu.VMEM)
    return pl.pallas_call(
        pack_kernel,
        in_specs=[vmem] * 5,
        out_specs=[vmem] * 2,
        out_shape=[
            jax.ShapeDtypeStruct((ROWS_F, 128), BF16),
            jax.ShapeDtypeStruct((ROWS_Q, 128), BF16),
        ],
        scratch_shapes=[pltpu.VMEM((ROWS_F, 128), F32), pltpu.VMEM((ROWS_Q, 128), F32)],
        name="pack",
    )(*pieces)


def lane_rows(v, rows, width):
    v = v.reshape(rows, width)
    full = -(-width // 128) * 128
    v = jnp.pad(v, ((0, 0), (0, full - width)))
    return v.reshape(rows * full // 128, 128)


def take_lanes(v, rows, width):
    full = -(-width // 128) * 128
    return v.reshape(rows, full)[:, :width].reshape(-1)


def rope_rows(v, cos_t, sin_t, heads, sign):
    out = []
    for head in range(heads):
        lo = v[head * HEAD : head * HEAD + 32]
        hi = v[head * HEAD + 32 : head * HEAD + 64]
        if sign > 0:
            out += [lo * cos_t - hi * sin_t, hi * cos_t + lo * sin_t]
        else:
            out += [lo * cos_t + hi * sin_t, hi * cos_t - lo * sin_t]
    return jnp.concatenate(out, axis=0)


def attn_fwd_kernel(
    pack_ref, x_ref, cos_ref, sin_ref, docr_ref, docc_ref,
    wqkv_ref, gain_ref, h_t_ref, q_t_ref, k_t_ref, v_t_ref, p_ref, o_t_ref,
    qs_ref, ks_ref, vs_ref, gs_ref, w_t_ref, bias_ref, k_ref,
):
    @pl.when(pl.program_id(0) == 0)
    def _():
        def squeeze(dev, carry):
            val = pack_ref[dev].astype(F32)
            put_rows(qs_ref, dev, R_OUT, val[Q_QUERY : Q_QUERY + R_OUT])
            put_rows(ks_ref, dev, R_KEY, val[Q_KEY : Q_KEY + R_KEY])
            put_rows(vs_ref, dev, R_KEY, val[Q_VALUE : Q_VALUE + R_KEY])
            put_rows(gs_ref, dev, 1, val[Q_GAIN : Q_GAIN + 1])
            return carry

        lax.fori_loop(0, 2 * CHIPS, squeeze, 0)
        parts = split_square(qs_ref)
        for ref in (ks_ref, vs_ref):
            for half in range(2):
                parts.append(ref[pl.ds(half, D, stride=2), :][:, :96])
        whole = jnp.concatenate(parts, axis=1)
        wqkv_ref[...] = whole.astype(BF16)
        w_t_ref[...] = whole.T.astype(BF16)
        for lane in range(9):
            gain_ref[pl.ds(lane, 2 * CHIPS, stride=9), :] = gs_ref[:, lane : lane + 1]

    x = x_ref[0].astype(F32)
    inv = lax.rsqrt(jnp.mean(x * x, axis=0, keepdims=True) + EPSILON)
    h_t = ((x * inv) * gain_ref[:D]).astype(BF16)
    h_t_ref[0] = h_t
    cos_t = cos_ref[0]
    sin_t = sin_ref[0]
    q_t = mm(w_t_ref[:D], h_t)
    q_t_ref[0] = rope_rows(q_t, cos_t, sin_t, HEADS, 1).astype(BF16) * 0.125
    k_t = rope_rows(mm(w_t_ref[D : D + KVW], h_t), cos_t, sin_t, KV_HEADS, 1).astype(BF16)
    k_t_ref[0] = k_t
    for group in range(KV_HEADS):
        k_ref[group] = k_t[group * HEAD : (group + 1) * HEAD].astype(F32).T.astype(BF16)
    v_t_ref[0] = mm(w_t_ref[D + KVW :], h_t).astype(BF16)
    key_at = lax.broadcasted_iota(jnp.int32, (SEQ, SEQ), 0)
    query_at = lax.broadcasted_iota(jnp.int32, (SEQ, SEQ), 1)
    same = docc_ref[0] == docr_ref[0]
    bias_ref[...] = jnp.where(same & (key_at <= query_at), 0.0, NEG_FILL)

    def group_step(group, carry):
        kv_rows = pl.ds(pl.multiple_of(group * HEAD, HEAD), HEAD)
        for member in range(HEADS // KV_HEADS):
            head = group * (HEADS // KV_HEADS) + member
            rows = pl.ds(pl.multiple_of(head * HEAD, HEAD), HEAD)
            for block in range(2):
                cols = slice(block * HALF, (block + 1) * HALF)
                keys = slice(0, (block + 1) * HALF)
                s_t = mm(k_ref[group, keys, :], q_t_ref[0, rows, cols]) + bias_ref[keys, cols]
                peak = jnp.max(s_t, axis=0, keepdims=True)
                e_t = jnp.exp(s_t - peak)
                scale = 1.0 / jnp.sum(e_t, axis=0, keepdims=True)
                p_t = (e_t * scale).astype(BF16)
                p_ref[0, head, keys, cols] = p_t
                o_t_ref[0, rows, cols] = mm(v_t_ref[0, kv_rows, keys], p_t).astype(BF16)
        return carry

    lax.fori_loop(0, KV_HEADS, group_step, 0)


def attn_fwd(pack_q, x_t, cos_t, sin_t, doc_row, doc_col):
    seqs = x_t.shape[0]
    out = [
        ((D, QKV), BF16, False),
        ((2 * D, 1), F32, False),
        ((D, SEQ), BF16, True),
        ((D, SEQ), BF16, True),
        ((KVW, SEQ), BF16, True),
        ((KVW, SEQ), BF16, True),
        ((HEADS, SEQ, SEQ), BF16, True),
        ((D, SEQ), BF16, True),
    ]
    return pl.pallas_call(
        attn_fwd_kernel,
        grid=(seqs,),
        in_specs=[
            whole_spec((2 * CHIPS, ROWS_Q, 128)),
            seq_spec((D, SEQ)),
            seq_spec((32, SEQ)),
            seq_spec((32, SEQ)),
            seq_spec((1, SEQ)),
            seq_spec((SEQ, 1)),
        ],
        out_specs=[seq_spec(s) if per else whole_spec(s) for s, _, per in out],
        out_shape=[jax.ShapeDtypeStruct(((seqs,) + s) if per else s, t) for s, t, per in out],
        scratch_shapes=[
            pltpu.VMEM((2 * CHIPS * R_OUT, 128), F32),
            pltpu.VMEM((2 * CHIPS * R_KEY, 128), F32),
            pltpu.VMEM((2 * CHIPS * R_KEY, 128), F32),
            pltpu.VMEM((2 * CHIPS, 128), F32),
            pltpu.VMEM((QKV, D), BF16),
            pltpu.VMEM((SEQ, SEQ), F32),
            pltpu.VMEM((KV_HEADS, SEQ, HEAD), BF16),
        ],
        compiler_params=pltpu.CompilerParams(vmem_limit_bytes=63 * 2**20),
        cost_estimate=pl.CostEstimate(
            flops=8 * 10**9, bytes_accessed=20 * 10**6, transcendentals=5 * 10**6
        ),
        name="attn_fwd",
    )(pack_q, x_t, cos_t, sin_t, doc_row, doc_col)


CHUNK = 256
CHUNKS = FF // CHUNK


def ffn_kernel(
    where_ref, pack_ref, x_ref, o_t_ref, cot_ref, gain_ref,
    y_ref, dx1_ref, do_t_ref, dgain_ref, send_g_ref, keep_g_ref, send_b_ref, keep_b_ref,
    gs_ref, us_ref, ds_ref, os_ref, wg_ref, wu_ref, wd_ref, wo_ref,
    acc_ref, h_t_ref, gb_ref, dh_ref, inv_ref, stage_ref,
):
    seqs = x_ref.shape[0]
    core = where_ref[0]

    def squeeze(dev, carry):
        val = pack_ref[dev].astype(F32)
        put_rows(gs_ref, dev, R_GATE, val[F_GATE : F_GATE + R_GATE])
        put_rows(us_ref, dev, R_GATE, val[F_UP : F_UP + R_GATE])
        put_rows(ds_ref, dev, R_DOWN, val[F_DOWN : F_DOWN + R_DOWN])
        put_rows(os_ref, dev, R_OUT, val[F_OUT : F_OUT + R_OUT])
        return carry

    lax.fori_loop(0, 2 * CHIPS, squeeze, 0)
    wo_ref[...] = jnp.concatenate(split_square(os_ref), axis=1).astype(BF16)
    for j in range(12):
        cols = slice(j * 128, (j + 1) * 128)
        wg_ref[:, cols] = gs_ref[pl.ds(j, D, stride=12), :].astype(BF16)
        wu_ref[:, cols] = us_ref[pl.ds(j, D, stride=12), :].astype(BF16)
    for j in range(5):
        width = min(128, D - j * 128)
        wd_ref[:, j * 128 : j * 128 + width] = ds_ref[pl.ds(j, FF, stride=5), :][:, :width].astype(BF16)

    gain = gain_ref[D:]
    for seq in range(seqs):
        cols = slice(seq * SEQ, (seq + 1) * SEQ)
        x1 = x_ref[seq].astype(F32) + mm(wo_ref[...], o_t_ref[seq], TN)
        inv = lax.rsqrt(jnp.mean(x1 * x1, axis=0, keepdims=True) + EPSILON)
        normed = x1 * inv
        acc_ref[:, cols] = x1
        inv_ref[:, cols] = inv
        dx1_ref[seq] = normed
        h_t_ref[:, cols] = (normed * gain).astype(BF16)
        gb_ref[:, cols] = cot_ref[seq].astype(BF16)
    dh_ref[...] = jnp.zeros_like(dh_ref)

    def chunk_step(chunk, carry):
        cols = pl.ds(pl.multiple_of(chunk * CHUNK, CHUNK), CHUNK)
        wg = wg_ref[:, cols]
        wu = wu_ref[:, cols]
        wd = wd_ref[cols, :]
        h_t = h_t_ref[...]
        gb = gb_ref[...]
        a = mm(wg, h_t, TN)
        b = mm(wu, h_t, TN)
        dm = mm(wd, gb)
        sg = 1.0 / (1.0 + jnp.exp(-a))
        silu = a * sg
        m = (silu * b).astype(BF16)
        da = (dm * b * sg * (1.0 + a * (1.0 - sg))).astype(BF16)
        db = (dm * silu).astype(BF16)
        acc_ref[...] += mm(wd, m, TN)
        dh_ref[...] += mm(wg, da) + mm(wu, db)
        dwg = mm(h_t, da, NT)
        dwu = mm(h_t, db, NT)
        dwd = mm(m, gb, NT)
        for j in range(CHUNK // 128):
            lane = slice(j * 128, (j + 1) * 128)
            at = chunk * (CHUNK // 128) + j
            gs_ref[pl.ds(at, D, stride=12), :] = dwg[:, lane]
            us_ref[pl.ds(at, D, stride=12), :] = dwu[:, lane]
        for j in range(5):
            width = min(128, D - j * 128)
            ds_ref[pl.ds(chunk * CHUNK * 5 + j, CHUNK, stride=5), :width] = dwd[
                :, j * 128 : j * 128 + width
            ]
        return carry

    lax.fori_loop(0, CHUNKS, chunk_step, 0)

    dgain = jnp.zeros((D, 1), F32)
    dwo = jnp.zeros((D, D), F32)
    for seq in range(seqs):
        cols = slice(seq * SEQ, (seq + 1) * SEQ)
        y_ref[seq] = acc_ref[:, cols].astype(BF16)
        dh = dh_ref[:, cols]
        normed = dx1_ref[seq]
        dgain += jnp.sum(dh * normed, axis=1, keepdims=True)
        dn = dh * gain
        dx1 = cot_ref[seq] + inv_ref[:, cols] * (
            dn - normed * jnp.mean(dn * normed, axis=0, keepdims=True)
        )
        dx1_ref[seq] = dx1
        low = dx1.astype(BF16)
        dwo += mm(o_t_ref[seq], low, NT)
        do_t_ref[seq] = mm(wo_ref[...], low).astype(BF16)
    dgain_ref[...] = dgain
    dh_ref[:, :D] = dwo
    join_square(os_ref, dh_ref)

    stage_ref[...] = jnp.zeros_like(stage_ref)

    def spread(slot, carry):
        for keep_it in range(2):
            chip = chip_of(slot, where_ref, False)
            dev = chip * 2 + (core if keep_it else 1 - core)
            stage_ref[G_DOWN : G_DOWN + R_DOWN, :] = get_rows(ds_ref, dev, R_DOWN)
            stage_ref[G_OUT : G_OUT + R_OUT, :] = get_rows(os_ref, dev, R_OUT)
            (keep_g_ref if keep_it else send_g_ref)[slot] = stage_ref[:ROWS_G].astype(BF16)
            chip = chip_of(slot, where_ref, True)
            dev = chip * 2 + (core if keep_it else 1 - core)
            stage_ref[B_GATE : B_GATE + R_GATE, :] = get_rows(gs_ref, dev, R_GATE)
            stage_ref[B_UP : B_UP + R_GATE, :] = get_rows(us_ref, dev, R_GATE)
            (keep_b_ref if keep_it else send_b_ref)[slot] = stage_ref[...].astype(BF16)
        return carry

    lax.fori_loop(0, CHIPS, spread, 0)


def ffn(where, pack_f, x_t, o_t, cot_t, gain):
    seqs = x_t.shape[0]
    cols_all = seqs * SEQ
    vmem = pl.BlockSpec(memory_space=pltpu.VMEM)
    return pl.pallas_call(
        ffn_kernel,
        in_specs=[pl.BlockSpec(memory_space=pltpu.SMEM)] + [vmem] * 5,
        out_specs=[vmem] * 8,
        out_shape=[
            jax.ShapeDtypeStruct((seqs, D, SEQ), BF16),
            jax.ShapeDtypeStruct((seqs, D, SEQ), F32),
            jax.ShapeDtypeStruct((seqs, D, SEQ), BF16),
            jax.ShapeDtypeStruct((D, 1), F32),
            jax.ShapeDtypeStruct((CHIPS, ROWS_G, 128), BF16),
            jax.ShapeDtypeStruct((CHIPS, ROWS_G, 128), BF16),
            jax.ShapeDtypeStruct((CHIPS, ROWS_B, 128), BF16),
            jax.ShapeDtypeStruct((CHIPS, ROWS_B, 128), BF16),
        ],
        scratch_shapes=[
            pltpu.VMEM((2 * CHIPS * R_GATE, 128), F32),
            pltpu.VMEM((2 * CHIPS * R_GATE, 128), F32),
            pltpu.VMEM((2 * CHIPS * R_DOWN, 128), F32),
            pltpu.VMEM((2 * CHIPS * R_OUT, 128), F32),
            pltpu.VMEM((D, FF), BF16),
            pltpu.VMEM((D, FF), BF16),
            pltpu.VMEM((FF, D), BF16),
            pltpu.VMEM((D, D), BF16),
            pltpu.VMEM((D, cols_all), F32),
            pltpu.VMEM((D, cols_all), BF16),
            pltpu.VMEM((D, cols_all), BF16),
            pltpu.VMEM((D, cols_all), F32),
            pltpu.VMEM((1, cols_all), F32),
            pltpu.VMEM((ROWS_B, 128), F32),
        ],
        compiler_params=pltpu.CompilerParams(vmem_limit_bytes=63 * 2**20),
        cost_estimate=pl.CostEstimate(
            flops=25 * 10**9, bytes_accessed=30 * 10**6, transcendentals=2 * 10**6
        ),
        name="ffn",
    )(where, pack_f, x_t, o_t, cot_t, gain)


def attn_bwd_kernel(
    cos_ref, sin_ref, q_t_ref, k_t_ref, v_t_ref, p_ref, o_t_ref, do_t_ref, *rest
):
    dqkv_ref, zero_ref, dq_ref, v_ref = rest[-4:]
    zero_ref[...] = jnp.zeros_like(zero_ref)
    for group in range(KV_HEADS):
        v_ref[group] = v_t_ref[0, group * HEAD : (group + 1) * HEAD, :].astype(F32).T.astype(BF16)

    def group_step(group, carry):
        kv_rows = pl.ds(pl.multiple_of(group * HEAD, HEAD), HEAD)
        dk = [jnp.zeros((HEAD, HALF), F32) for _ in range(2)]
        dv = [jnp.zeros((HEAD, HALF), F32) for _ in range(2)]
        for member in range(HEADS // KV_HEADS):
            head = group * (HEADS // KV_HEADS) + member
            rows = pl.ds(pl.multiple_of(head * HEAD, HEAD), HEAD)
            for block in range(2):
                cols = slice(block * HALF, (block + 1) * HALF)
                keys = slice(0, (block + 1) * HALF)
                do_t = do_t_ref[0, rows, cols]
                q_t = q_t_ref[0, rows, cols]
                p_t = p_ref[0, head, keys, cols]
                row_sum = jnp.sum(
                    do_t.astype(F32) * o_t_ref[0, rows, cols].astype(F32), axis=0, keepdims=True
                )
                dp_t = mm(v_ref[group, keys, :], do_t)
                ds_t = (p_t.astype(F32) * (dp_t - row_sum)).astype(BF16)
                dq_ref[rows, cols] = mm(k_t_ref[0, kv_rows, keys], ds_t) * 0.125
                dk_new = mm(q_t, ds_t, NT)
                dv_new = mm(do_t, p_t, NT)
                for part in range(block + 1):
                    at = slice(part * HALF, (part + 1) * HALF)
                    dk[part] += dk_new[:, at]
                    dv[part] += dv_new[:, at]
        dq_ref[pl.ds(pl.multiple_of(D + group * HEAD, HEAD), HEAD), :] = jnp.concatenate(dk, axis=1)
        dqkv_ref[pl.ds(pl.multiple_of(D + KVW + group * HEAD, HEAD), HEAD), :] = jnp.concatenate(
            dv, axis=1
        ).astype(BF16)
        return carry

    lax.fori_loop(0, KV_HEADS, group_step, 0)
    dqkv_ref[: D + KVW] = rope_rows(
        dq_ref[...], cos_ref[0], sin_ref[0], HEADS + KV_HEADS, -1
    ).astype(BF16)


def attn_bwd(seq, args, after):
    return pl.pallas_call(
        attn_bwd_kernel,
        grid=(1,),
        in_specs=[
            seq_spec((32, SEQ), seq),
            seq_spec((32, SEQ), seq),
            seq_spec((D, SEQ), seq),
            seq_spec((KVW, SEQ), seq),
            seq_spec((KVW, SEQ), seq),
            seq_spec((HEADS, SEQ, SEQ), seq),
            seq_spec((D, SEQ), seq),
            seq_spec((D, SEQ), seq),
        ]
        + [pl.BlockSpec(memory_space=pl.ANY)] * len(after),
        out_specs=[whole_spec((QKV, SEQ)), whole_spec((8, 128))],
        out_shape=[
            jax.ShapeDtypeStruct((QKV, SEQ), BF16),
            jax.ShapeDtypeStruct((8, 128), F32),
        ],
        scratch_shapes=[
            pltpu.VMEM((D + KVW, SEQ), F32),
            pltpu.VMEM((KV_HEADS, SEQ, HEAD), BF16),
        ],
        compiler_params=pltpu.CompilerParams(vmem_limit_bytes=(63 if seq == 0 else 40) * 2**20),
        cost_estimate=pl.CostEstimate(flops=8 * 10**9, bytes_accessed=8 * 10**6, transcendentals=0),
        name="attn_bwd",
    )(*args, *after)


def qkv_bwd_kernel(
    where_ref, w_ref, gain_ref, dgain_two_ref, x_ref, h_t_ref, dx1_ref, dqkv0_ref, dqkv1_ref, *rest
):
    gx_ref, send_ref, keep_ref, zero_ref = rest[-11:-7]
    dw_ref, dgain_ref, qs_ref, ks_ref, vs_ref, gs_ref, stage_ref = rest[-7:]
    zero_ref[...] = jnp.zeros_like(zero_ref)
    dw = jnp.zeros((D, QKV), F32)
    dgain = jnp.zeros((D, 1), F32)
    for seq, dqkv_ref in enumerate((dqkv0_ref, dqkv1_ref)):
        dqkv = dqkv_ref[...]
        dh = mm(w_ref[...], dqkv)
        dw += mm(h_t_ref[seq], dqkv, NT)
        x = x_ref[seq].astype(F32)
        inv = lax.rsqrt(jnp.mean(x * x, axis=0, keepdims=True) + EPSILON)
        normed = x * inv
        dn = dh * gain_ref[:D]
        gx_ref[seq] = dx1_ref[seq] + inv * (
            dn - normed * jnp.mean(dn * normed, axis=0, keepdims=True)
        )
        dgain += jnp.sum(dh * normed, axis=1, keepdims=True)
    dw_ref[...] = dw
    dgain_ref[:D] = dgain
    dgain_ref[D:] = dgain_two_ref[...]
    join_square(qs_ref, dw_ref)
    for half in range(2):
        at = D + 96 * half
        ks_ref[pl.ds(half, D, stride=2), :96] = dw_ref[:, at : at + 96]
        vs_ref[pl.ds(half, D, stride=2), :96] = dw_ref[:, at + KVW : at + KVW + 96]
    for lane in range(9):
        gs_ref[:, lane : lane + 1] = dgain_ref[pl.ds(lane, 2 * CHIPS, stride=9), :]
    core = where_ref[0]
    stage_ref[...] = jnp.zeros_like(stage_ref)

    def spread(slot, carry):
        chip = chip_of(slot, where_ref, False)
        for keep_it in range(2):
            dev = chip * 2 + (core if keep_it else 1 - core)
            stage_ref[Q_QUERY : Q_QUERY + R_OUT, :] = get_rows(qs_ref, dev, R_OUT)
            stage_ref[Q_KEY : Q_KEY + R_KEY, :] = get_rows(ks_ref, dev, R_KEY)
            stage_ref[Q_VALUE : Q_VALUE + R_KEY, :] = get_rows(vs_ref, dev, R_KEY)
            stage_ref[Q_GAIN : Q_GAIN + 1, :] = get_rows(gs_ref, dev, 1)
            (keep_ref if keep_it else send_ref)[slot] = stage_ref[...].astype(BF16)
        return carry

    lax.fori_loop(0, CHIPS, spread, 0)


def qkv_bwd(args, after):
    seqs = args[4].shape[0]
    vmem = pl.BlockSpec(memory_space=pltpu.VMEM)
    return pl.pallas_call(
        qkv_bwd_kernel,
        in_specs=[pl.BlockSpec(memory_space=pltpu.SMEM)]
        + [vmem] * (len(args) - 1)
        + [pl.BlockSpec(memory_space=pl.ANY)] * len(after),
        out_specs=[vmem] * 4,
        out_shape=[
            jax.ShapeDtypeStruct((seqs, D, SEQ), F32),
            jax.ShapeDtypeStruct((CHIPS, ROWS_Q, 128), BF16),
            jax.ShapeDtypeStruct((CHIPS, ROWS_Q, 128), BF16),
            jax.ShapeDtypeStruct((8, 128), F32),
        ],
        scratch_shapes=[
            pltpu.VMEM((D, QKV), F32),
            pltpu.VMEM((2 * D, 1), F32),
            pltpu.VMEM((2 * CHIPS * R_OUT, 128), F32),
            pltpu.VMEM((2 * CHIPS * R_KEY, 128), F32),
            pltpu.VMEM((2 * CHIPS * R_KEY, 128), F32),
            pltpu.VMEM((2 * CHIPS, 128), F32),
            pltpu.VMEM((ROWS_Q, 128), F32),
        ],
        compiler_params=pltpu.CompilerParams(vmem_limit_bytes=40 * 2**20),
        cost_estimate=pl.CostEstimate(flops=8 * 10**9, bytes_accessed=12 * 10**6, transcendentals=0),
        name="qkv_bwd",
    )(*args, *after)


def pairs(axis, step):
    out = []
    for x in range(4):
        for y in range(4):
            for z in range(4):
                for core in range(2):
                    to = {"x": x, "y": y, "z": z, "c": core}
                    to[axis] = (to[axis] + step) % (2 if axis == "c" else 4)
                    me = ((x * 4 + y) * 4 + z) * 2 + core
                    out.append((me, ((to["x"] * 4 + to["y"]) * 4 + to["z"]) * 2 + to["c"]))
    return out


def hop(v, axis, step):
    return lax.ppermute(v, "dp", pairs(axis, step))


def sum_near(v, axis):
    low = v[1:].astype(BF16)
    got = [hop(low[k - 1], axis, k) for k in (2, 1, 3)]
    total = v[0].astype(F32)
    for piece in got:
        total = total + piece.astype(F32)
    return total


def both(keep, got, place, zero):
    rows = keep.shape[1]
    keep = keep.reshape(4, 4, 4, rows, 128)[place]
    got = got.reshape(4, 4, 4, rows, 128)[place]
    return keep.astype(F32) + got.astype(F32) + zero[0, 0]


def ring_far(far, axis):
    return hop(far[:2], axis, 1).astype(F32), hop(far[2:], axis, 3).astype(F32)


def ring_near(keep, got, arrived, zero):
    ahead, behind = both(keep, got, 1, zero), both(keep, got, 3, zero)
    ahead = jnp.concatenate([ahead[:2] + arrived[0], ahead[2:]])
    behind = jnp.concatenate([behind[:2], behind[2:] + arrived[1]])
    return ahead.astype(BF16), behind.astype(BF16)


def on_device(
    tokens, positions, norm_gains, w_query, w_key, w_value, w_out, w_gate, w_up, w_down, cotangent
):
    me = lax.axis_index("dp").astype(jnp.int32)
    where = jnp.stack([me % 2, me // 32, (me // 8) % 4, (me // 2) % 4])
    seqs = tokens.shape[0]
    x_t = jnp.swapaxes(tokens, 1, 2)
    cot_t = jnp.swapaxes(cotangent, 1, 2)

    pack_f, pack_q = pack(
        [
            lane_rows(jnp.concatenate([w_query, w_out]), 18, 288),
            jnp.concatenate([w_key, w_value]).reshape(18, 96),
            norm_gains.reshape(1, 9),
            lane_rows(w_down, 12, D),
            jnp.concatenate([w_gate, w_up]).reshape(2 * R_GATE, 128),
        ]
    )
    all_f = lax.all_gather(pack_f, "dp", axis=0, tiled=False)
    all_q = lax.all_to_all(
        jnp.broadcast_to(pack_q[None], (2 * CHIPS, ROWS_Q, 128)), "dp", split_axis=0, concat_axis=0
    )

    freqs = 100000.0 ** (-(jnp.arange(HEAD // 2, dtype=F32) * 2.0 / HEAD))
    angles = positions.astype(F32)[:, None, :] * freqs[None, :, None]
    cos_t = jnp.cos(angles)
    sin_t = jnp.sin(angles)
    fresh = (positions[:, 1:] != positions[:, :-1] + 1).astype(jnp.int32)
    docs = jnp.cumsum(jnp.pad(fresh, ((0, 0), (1, 0))), axis=1)

    wqkv, gain, h_t, q_t, k_t, v_t, p, o_t = attn_fwd(
        all_q, x_t, cos_t, sin_t, docs[:, None, :], docs[:, :, None]
    )
    y_t, dx1, do_t, dgain_two, send_g, keep_g, send_b, keep_b = ffn(
        where, all_f, x_t, o_t, cot_t, gain
    )
    got_g = hop(send_g, "c", 1)
    got_b = hop(send_b, "c", 1)
    args = [cos_t, sin_t, q_t, k_t, v_t, p, o_t, do_t]
    dqkv0, zero = attn_bwd(0, args, [])
    far_g = both(keep_g, got_g, 2, zero).astype(BF16)
    far_b = both(keep_b, got_b, 2, zero).astype(BF16)
    dqkv1, zero = attn_bwd(1, args, [far_g, far_b])
    near_g = ring_near(keep_g, got_g, ring_far(far_g, "z"), zero)
    near_b = ring_near(keep_b, got_b, ring_far(far_b, "y"), zero)
    gx_t, send_q, keep_q, zero = qkv_bwd(
        [where, wqkv, gain, dgain_two, x_t, h_t, dx1, dqkv0, dqkv1], near_g + near_b
    )
    got_q = hop(send_q, "c", 1)
    sum_g = both(keep_g, got_g, 0, zero)
    sum_g = sum_g + hop(near_g[0], "z", 1).astype(F32) + hop(near_g[1], "z", 3).astype(F32)
    sum_b = both(keep_b, got_b, 0, zero)
    sum_b = sum_b + hop(near_b[0], "y", 1).astype(F32) + hop(near_b[1], "y", 3).astype(F32)
    sum_q = (keep_q.astype(F32) + got_q.astype(F32)).reshape(4, 4, 4, ROWS_Q, 128)
    sum_q = sum_near(sum_q, "z")
    sum_b = sum_near(sum_b, "z")
    sum_a = sum_near(jnp.concatenate([sum_g, sum_q], axis=2), "y")
    final = sum_near(jnp.concatenate([sum_a, sum_b], axis=1), "x")
    fg = final[:ROWS_G]
    fq = final[ROWS_G : ROWS_G + ROWS_Q]
    fb = final[ROWS_G + ROWS_Q :]
    return (
        jnp.swapaxes(y_t, 1, 2),
        jnp.swapaxes(gx_t, 1, 2),
        take_lanes(fq[Q_GAIN : Q_GAIN + 1], 1, 9),
        take_lanes(fq[Q_QUERY : Q_QUERY + R_OUT], 9, 288),
        take_lanes(fq[Q_KEY : Q_KEY + R_KEY], 9, 96),
        take_lanes(fq[Q_VALUE : Q_VALUE + R_KEY], 9, 96),
        take_lanes(fg[G_OUT : G_OUT + R_OUT], 9, 288),
        fb[B_GATE : B_GATE + R_GATE].reshape(-1),
        fb[B_UP : B_UP + R_GATE].reshape(-1),
        take_lanes(fg[G_DOWN : G_DOWN + R_DOWN], 12, D),
    )


def solution(mesh):
    flat = P("dp")
    cube = P("dp", None, None)
    return jax.shard_map(
        on_device,
        mesh=mesh,
        in_specs=(cube, P("dp", None)) + (flat,) * 8 + (cube,),
        out_specs=(cube, cube) + (flat,) * 8,
        check_vma=False,
    )
```

```python
import functools

import jax
import jax.numpy as jnp
from jax import lax
from jax.sharding import PartitionSpec as P
from jax.experimental import pallas as pl
from jax.experimental.pallas import tpu as pltpu

D = 576
HEADS = 9
KV_HEADS = 3
HEAD = 64
FF = 1536
SEQ = 512
KVW = KV_HEADS * HEAD
QKV = D + 2 * KVW
HALF = SEQ // 2

EPSILON = 1e-05
NEG_FILL = -1e30

F32 = jnp.float32
BF16 = jnp.bfloat16

CHIPS = 64
R_GATE = 54
R_DOWN = 60
R_OUT = 27
R_KEY = 9
F_GATE, F_UP, F_DOWN, F_OUT, ROWS_F = 0, 54, 112, 172, 208
B_GATE, B_UP, ROWS_B = 0, 54, 112
G_DOWN, G_OUT, ROWS_G = 0, 60, 96
Q_QUERY, Q_KEY, Q_VALUE, Q_GAIN, ROWS_Q = 0, 27, 36, 45, 48

NN = (((1,), (0,)), ((), ()))
NT = (((1,), (1,)), ((), ()))
TN = (((0,), (0,)), ((), ()))


def mm(a, b, dims=NN):
    return lax.dot_general(a, b, dims, preferred_element_type=F32)


def whole_spec(shape):
    zeros = (0,) * len(shape)
    return pl.BlockSpec(shape, lambda i: zeros)


def seq_spec(shape, at=None):
    zeros = (0,) * len(shape)
    return pl.BlockSpec((1,) + shape, lambda i: (i if at is None else at,) + zeros)


def chip_of(slot, where_ref, swap):
    one, two, three = slot // 16, (slot // 4) % 4, slot % 4
    kz, ky = (two, one) if swap else (one, two)
    x = (where_ref[1] + three) % 4
    y = (where_ref[2] + ky) % 4
    z = (where_ref[3] + kz) % 4
    return (x * 4 + y) * 4 + z


def put_rows(ref, dev, rows, val):
    ref[pl.ds(dev * rows, rows), :] = val


def get_rows(ref, dev, rows):
    return ref[pl.ds(dev * rows, rows), :]


def split_square(ref):
    parts = []
    for half in range(2):
        for j in range(3):
            piece = ref[pl.ds(3 * half + j, D, stride=6), :]
            parts.append(piece if j < 2 else piece[:, :32])
    return parts


def join_square(ref, val_ref):
    for half in range(2):
        for j in range(3):
            width = 128 if j < 2 else 32
            at = 288 * half + 128 * j
            ref[pl.ds(3 * half + j, D, stride=6), :width] = val_ref[:, at : at + width]


def pack_kernel(starts, count, *refs):
    out_ref, stage_ref = refs[-2:]
    stage_ref[...] = jnp.zeros_like(stage_ref)
    for at, ref in zip(starts, refs[:count]):
        val = ref[...].astype(F32)
        stage_ref[at : at + val.shape[0], : val.shape[1]] = val
    out_ref[...] = stage_ref[...].astype(BF16)


def pack(pieces, starts, rows, after):
    vmem = pl.BlockSpec(memory_space=pltpu.VMEM)
    return pl.pallas_call(
        functools.partial(pack_kernel, starts, len(pieces)),
        in_specs=[vmem] * len(pieces) + [pl.BlockSpec(memory_space=pl.ANY)] * len(after),
        out_specs=vmem,
        out_shape=jax.ShapeDtypeStruct((rows, 128), BF16),
        scratch_shapes=[pltpu.VMEM((rows, 128), F32)],
        name="pack",
    )(*pieces, *after)


def lane_rows(v, rows, width):
    v = v.reshape(rows, width)
    full = -(-width // 128) * 128
    v = jnp.pad(v, ((0, 0), (0, full - width)))
    return v.reshape(rows * full // 128, 128)


def take_lanes(v, rows, width):
    full = -(-width // 128) * 128
    return v.reshape(rows, full)[:, :width].reshape(-1)


def rope_rows(v, cos_t, sin_t, heads, sign):
    out = []
    for head in range(heads):
        lo = v[head * HEAD : head * HEAD + 32]
        hi = v[head * HEAD + 32 : head * HEAD + 64]
        if sign > 0:
            out += [lo * cos_t - hi * sin_t, hi * cos_t + lo * sin_t]
        else:
            out += [lo * cos_t + hi * sin_t, hi * cos_t - lo * sin_t]
    return jnp.concatenate(out, axis=0)


def attn_fwd_kernel(
    pack_ref, x_ref, cos_ref, sin_ref, docr_ref, docc_ref,
    wqkv_ref, gain_ref, h_t_ref, q_t_ref, k_t_ref, v_t_ref, p_ref, o_t_ref,
    qs_ref, ks_ref, vs_ref, gs_ref, w_t_ref, bias_ref, k_ref,
):
    @pl.when(pl.program_id(0) == 0)
    def _():
        def squeeze(dev, carry):
            val = pack_ref[dev].astype(F32)
            put_rows(qs_ref, dev, R_OUT, val[Q_QUERY : Q_QUERY + R_OUT])
            put_rows(ks_ref, dev, R_KEY, val[Q_KEY : Q_KEY + R_KEY])
            put_rows(vs_ref, dev, R_KEY, val[Q_VALUE : Q_VALUE + R_KEY])
            put_rows(gs_ref, dev, 1, val[Q_GAIN : Q_GAIN + 1])
            return carry

        lax.fori_loop(0, 2 * CHIPS, squeeze, 0)
        parts = split_square(qs_ref)
        for ref in (ks_ref, vs_ref):
            for half in range(2):
                parts.append(ref[pl.ds(half, D, stride=2), :][:, :96])
        whole = jnp.concatenate(parts, axis=1)
        wqkv_ref[...] = whole.astype(BF16)
        w_t_ref[...] = whole.T.astype(BF16)
        for lane in range(9):
            gain_ref[pl.ds(lane, 2 * CHIPS, stride=9), :] = gs_ref[:, lane : lane + 1]

    x = x_ref[0].astype(F32)
    inv = lax.rsqrt(jnp.mean(x * x, axis=0, keepdims=True) + EPSILON)
    h_t = ((x * inv) * gain_ref[:D]).astype(BF16)
    h_t_ref[0] = h_t
    cos_t = cos_ref[0]
    sin_t = sin_ref[0]
    q_t = mm(w_t_ref[:D], h_t)
    q_t_ref[0] = rope_rows(q_t, cos_t, sin_t, HEADS, 1).astype(BF16) * 0.125
    k_t = rope_rows(mm(w_t_ref[D : D + KVW], h_t), cos_t, sin_t, KV_HEADS, 1).astype(BF16)
    k_t_ref[0] = k_t
    for group in range(KV_HEADS):
        k_ref[group] = k_t[group * HEAD : (group + 1) * HEAD].astype(F32).T.astype(BF16)
    v_t_ref[0] = mm(w_t_ref[D + KVW :], h_t).astype(BF16)
    key_at = lax.broadcasted_iota(jnp.int32, (SEQ, SEQ), 0)
    query_at = lax.broadcasted_iota(jnp.int32, (SEQ, SEQ), 1)
    same = docc_ref[0] == docr_ref[0]
    bias_ref[...] = jnp.where(same & (key_at <= query_at), 0.0, NEG_FILL)

    def group_step(group, carry):
        kv_rows = pl.ds(pl.multiple_of(group * HEAD, HEAD), HEAD)
        for member in range(HEADS // KV_HEADS):
            head = group * (HEADS // KV_HEADS) + member
            rows = pl.ds(pl.multiple_of(head * HEAD, HEAD), HEAD)
            for block in range(2):
                cols = slice(block * HALF, (block + 1) * HALF)
                keys = slice(0, (block + 1) * HALF)
                s_t = mm(k_ref[group, keys, :], q_t_ref[0, rows, cols]) + bias_ref[keys, cols]
                peak = jnp.max(s_t, axis=0, keepdims=True)
                e_t = jnp.exp(s_t - peak)
                scale = 1.0 / jnp.sum(e_t, axis=0, keepdims=True)
                p_t = (e_t * scale).astype(BF16)
                p_ref[0, head, keys, cols] = p_t
                o_t_ref[0, rows, cols] = mm(v_t_ref[0, kv_rows, keys], p_t).astype(BF16)
        return carry

    lax.fori_loop(0, KV_HEADS, group_step, 0)


def attn_fwd(pack_q, x_t, cos_t, sin_t, doc_row, doc_col):
    seqs = x_t.shape[0]
    out = [
        ((D, QKV), BF16, False),
        ((2 * D, 1), F32, False),
        ((D, SEQ), BF16, True),
        ((D, SEQ), BF16, True),
        ((KVW, SEQ), BF16, True),
        ((KVW, SEQ), BF16, True),
        ((HEADS, SEQ, SEQ), BF16, True),
        ((D, SEQ), BF16, True),
    ]
    return pl.pallas_call(
        attn_fwd_kernel,
        grid=(seqs,),
        in_specs=[
            whole_spec((2 * CHIPS, ROWS_Q, 128)),
            seq_spec((D, SEQ)),
            seq_spec((32, SEQ)),
            seq_spec((32, SEQ)),
            seq_spec((1, SEQ)),
            seq_spec((SEQ, 1)),
        ],
        out_specs=[seq_spec(s) if per else whole_spec(s) for s, _, per in out],
        out_shape=[jax.ShapeDtypeStruct(((seqs,) + s) if per else s, t) for s, t, per in out],
        scratch_shapes=[
            pltpu.VMEM((2 * CHIPS * R_OUT, 128), F32),
            pltpu.VMEM((2 * CHIPS * R_KEY, 128), F32),
            pltpu.VMEM((2 * CHIPS * R_KEY, 128), F32),
            pltpu.VMEM((2 * CHIPS, 128), F32),
            pltpu.VMEM((QKV, D), BF16),
            pltpu.VMEM((SEQ, SEQ), F32),
            pltpu.VMEM((KV_HEADS, SEQ, HEAD), BF16),
        ],
        compiler_params=pltpu.CompilerParams(vmem_limit_bytes=63 * 2**20),
        cost_estimate=pl.CostEstimate(
            flops=8 * 10**9, bytes_accessed=20 * 10**6, transcendentals=5 * 10**6
        ),
        name="attn_fwd",
    )(pack_q, x_t, cos_t, sin_t, doc_row, doc_col)


CHUNK = 256
CHUNKS = FF // CHUNK


def ffn_kernel(
    where_ref, pack_ref, x_ref, o_t_ref, cot_ref, gain_ref,
    y_ref, dx1_ref, do_t_ref, dgain_ref, send_g_ref, keep_g_ref, send_b_ref, keep_b_ref,
    gs_ref, us_ref, ds_ref, os_ref, wg_ref, wu_ref, wd_ref, wo_ref,
    acc_ref, h_t_ref, gb_ref, dh_ref, inv_ref, stage_ref,
):
    seqs = x_ref.shape[0]
    core = where_ref[0]

    def squeeze(dev, carry):
        val = pack_ref[dev].astype(F32)
        put_rows(gs_ref, dev, R_GATE, val[F_GATE : F_GATE + R_GATE])
        put_rows(us_ref, dev, R_GATE, val[F_UP : F_UP + R_GATE])
        put_rows(ds_ref, dev, R_DOWN, val[F_DOWN : F_DOWN + R_DOWN])
        put_rows(os_ref, dev, R_OUT, val[F_OUT : F_OUT + R_OUT])
        return carry

    lax.fori_loop(0, 2 * CHIPS, squeeze, 0)
    wo_ref[...] = jnp.concatenate(split_square(os_ref), axis=1).astype(BF16)
    for j in range(12):
        cols = slice(j * 128, (j + 1) * 128)
        wg_ref[:, cols] = gs_ref[pl.ds(j, D, stride=12), :].astype(BF16)
        wu_ref[:, cols] = us_ref[pl.ds(j, D, stride=12), :].astype(BF16)
    for j in range(5):
        width = min(128, D - j * 128)
        wd_ref[:, j * 128 : j * 128 + width] = ds_ref[pl.ds(j, FF, stride=5), :][:, :width].astype(BF16)

    gain = gain_ref[D:]
    for seq in range(seqs):
        cols = slice(seq * SEQ, (seq + 1) * SEQ)
        x1 = x_ref[seq].astype(F32) + mm(wo_ref[...], o_t_ref[seq], TN)
        inv = lax.rsqrt(jnp.mean(x1 * x1, axis=0, keepdims=True) + EPSILON)
        normed = x1 * inv
        acc_ref[:, cols] = x1
        inv_ref[:, cols] = inv
        dx1_ref[seq] = normed
        h_t_ref[:, cols] = (normed * gain).astype(BF16)
        gb_ref[:, cols] = cot_ref[seq].astype(BF16)
    dh_ref[...] = jnp.zeros_like(dh_ref)

    def chunk_step(chunk, carry):
        cols = pl.ds(pl.multiple_of(chunk * CHUNK, CHUNK), CHUNK)
        wg = wg_ref[:, cols]
        wu = wu_ref[:, cols]
        wd = wd_ref[cols, :]
        h_t = h_t_ref[...]
        gb = gb_ref[...]
        a = mm(wg, h_t, TN)
        b = mm(wu, h_t, TN)
        dm = mm(wd, gb)
        sg = 1.0 / (1.0 + jnp.exp(-a))
        silu = a * sg
        m = (silu * b).astype(BF16)
        da = (dm * b * sg * (1.0 + a * (1.0 - sg))).astype(BF16)
        db = (dm * silu).astype(BF16)
        acc_ref[...] += mm(wd, m, TN)
        dh_ref[...] += mm(wg, da) + mm(wu, db)
        dwg = mm(h_t, da, NT)
        dwu = mm(h_t, db, NT)
        dwd = mm(m, gb, NT)
        for j in range(CHUNK // 128):
            lane = slice(j * 128, (j + 1) * 128)
            at = chunk * (CHUNK // 128) + j
            gs_ref[pl.ds(at, D, stride=12), :] = dwg[:, lane]
            us_ref[pl.ds(at, D, stride=12), :] = dwu[:, lane]
        for j in range(5):
            width = min(128, D - j * 128)
            ds_ref[pl.ds(chunk * CHUNK * 5 + j, CHUNK, stride=5), :width] = dwd[
                :, j * 128 : j * 128 + width
            ]
        return carry

    lax.fori_loop(0, CHUNKS, chunk_step, 0)

    dgain = jnp.zeros((D, 1), F32)
    dwo = jnp.zeros((D, D), F32)
    for seq in range(seqs):
        cols = slice(seq * SEQ, (seq + 1) * SEQ)
        y_ref[seq] = acc_ref[:, cols].astype(BF16)
        dh = dh_ref[:, cols]
        normed = dx1_ref[seq]
        dgain += jnp.sum(dh * normed, axis=1, keepdims=True)
        dn = dh * gain
        dx1 = cot_ref[seq] + inv_ref[:, cols] * (
            dn - normed * jnp.mean(dn * normed, axis=0, keepdims=True)
        )
        dx1_ref[seq] = dx1
        low = dx1.astype(BF16)
        dwo += mm(o_t_ref[seq], low, NT)
        do_t_ref[seq] = mm(wo_ref[...], low).astype(BF16)
    dgain_ref[...] = dgain
    dh_ref[:, :D] = dwo
    join_square(os_ref, dh_ref)

    stage_ref[...] = jnp.zeros_like(stage_ref)

    def spread(slot, carry):
        for keep_it in range(2):
            chip = chip_of(slot, where_ref, False)
            dev = chip * 2 + (core if keep_it else 1 - core)
            stage_ref[G_DOWN : G_DOWN + R_DOWN, :] = get_rows(ds_ref, dev, R_DOWN)
            stage_ref[G_OUT : G_OUT + R_OUT, :] = get_rows(os_ref, dev, R_OUT)
            (keep_g_ref if keep_it else send_g_ref)[slot] = stage_ref[:ROWS_G].astype(BF16)
            chip = chip_of(slot, where_ref, True)
            dev = chip * 2 + (core if keep_it else 1 - core)
            stage_ref[B_GATE : B_GATE + R_GATE, :] = get_rows(gs_ref, dev, R_GATE)
            stage_ref[B_UP : B_UP + R_GATE, :] = get_rows(us_ref, dev, R_GATE)
            (keep_b_ref if keep_it else send_b_ref)[slot] = stage_ref[...].astype(BF16)
        return carry

    lax.fori_loop(0, CHIPS, spread, 0)


def ffn(where, pack_f, x_t, o_t, cot_t, gain):
    seqs = x_t.shape[0]
    cols_all = seqs * SEQ
    vmem = pl.BlockSpec(memory_space=pltpu.VMEM)
    return pl.pallas_call(
        ffn_kernel,
        in_specs=[pl.BlockSpec(memory_space=pltpu.SMEM)] + [vmem] * 5,
        out_specs=[vmem] * 8,
        out_shape=[
            jax.ShapeDtypeStruct((seqs, D, SEQ), BF16),
            jax.ShapeDtypeStruct((seqs, D, SEQ), F32),
            jax.ShapeDtypeStruct((seqs, D, SEQ), BF16),
            jax.ShapeDtypeStruct((D, 1), F32),
            jax.ShapeDtypeStruct((CHIPS, ROWS_G, 128), BF16),
            jax.ShapeDtypeStruct((CHIPS, ROWS_G, 128), BF16),
            jax.ShapeDtypeStruct((CHIPS, ROWS_B, 128), BF16),
            jax.ShapeDtypeStruct((CHIPS, ROWS_B, 128), BF16),
        ],
        scratch_shapes=[
            pltpu.VMEM((2 * CHIPS * R_GATE, 128), F32),
            pltpu.VMEM((2 * CHIPS * R_GATE, 128), F32),
            pltpu.VMEM((2 * CHIPS * R_DOWN, 128), F32),
            pltpu.VMEM((2 * CHIPS * R_OUT, 128), F32),
            pltpu.VMEM((D, FF), BF16),
            pltpu.VMEM((D, FF), BF16),
            pltpu.VMEM((FF, D), BF16),
            pltpu.VMEM((D, D), BF16),
            pltpu.VMEM((D, cols_all), F32),
            pltpu.VMEM((D, cols_all), BF16),
            pltpu.VMEM((D, cols_all), BF16),
            pltpu.VMEM((D, cols_all), F32),
            pltpu.VMEM((1, cols_all), F32),
            pltpu.VMEM((ROWS_B, 128), F32),
        ],
        compiler_params=pltpu.CompilerParams(vmem_limit_bytes=63 * 2**20),
        cost_estimate=pl.CostEstimate(
            flops=25 * 10**9, bytes_accessed=30 * 10**6, transcendentals=2 * 10**6
        ),
        name="ffn",
    )(where, pack_f, x_t, o_t, cot_t, gain)


def attn_bwd_kernel(
    cos_ref, sin_ref, q_t_ref, k_t_ref, v_t_ref, p_ref, o_t_ref, do_t_ref, *rest
):
    dqkv_ref, zero_ref, dq_ref, v_ref = rest[-4:]
    zero_ref[...] = jnp.zeros_like(zero_ref)
    for group in range(KV_HEADS):
        v_ref[group] = v_t_ref[0, group * HEAD : (group + 1) * HEAD, :].astype(F32).T.astype(BF16)

    def group_step(group, carry):
        kv_rows = pl.ds(pl.multiple_of(group * HEAD, HEAD), HEAD)
        dk = [jnp.zeros((HEAD, HALF), F32) for _ in range(2)]
        dv = [jnp.zeros((HEAD, HALF), F32) for _ in range(2)]
        for member in range(HEADS // KV_HEADS):
            head = group * (HEADS // KV_HEADS) + member
            rows = pl.ds(pl.multiple_of(head * HEAD, HEAD), HEAD)
            for block in range(2):
                cols = slice(block * HALF, (block + 1) * HALF)
                keys = slice(0, (block + 1) * HALF)
                do_t = do_t_ref[0, rows, cols]
                q_t = q_t_ref[0, rows, cols]
                p_t = p_ref[0, head, keys, cols]
                row_sum = jnp.sum(
                    do_t.astype(F32) * o_t_ref[0, rows, cols].astype(F32), axis=0, keepdims=True
                )
                dp_t = mm(v_ref[group, keys, :], do_t)
                ds_t = (p_t.astype(F32) * (dp_t - row_sum)).astype(BF16)
                dq_ref[rows, cols] = mm(k_t_ref[0, kv_rows, keys], ds_t) * 0.125
                dk_new = mm(q_t, ds_t, NT)
                dv_new = mm(do_t, p_t, NT)
                for part in range(block + 1):
                    at = slice(part * HALF, (part + 1) * HALF)
                    dk[part] += dk_new[:, at]
                    dv[part] += dv_new[:, at]
        dq_ref[pl.ds(pl.multiple_of(D + group * HEAD, HEAD), HEAD), :] = jnp.concatenate(dk, axis=1)
        dqkv_ref[pl.ds(pl.multiple_of(D + KVW + group * HEAD, HEAD), HEAD), :] = jnp.concatenate(
            dv, axis=1
        ).astype(BF16)
        return carry

    lax.fori_loop(0, KV_HEADS, group_step, 0)
    dqkv_ref[: D + KVW] = rope_rows(
        dq_ref[...], cos_ref[0], sin_ref[0], HEADS + KV_HEADS, -1
    ).astype(BF16)


def attn_bwd(seq, args, after):
    return pl.pallas_call(
        attn_bwd_kernel,
        grid=(1,),
        in_specs=[
            seq_spec((32, SEQ), seq),
            seq_spec((32, SEQ), seq),
            seq_spec((D, SEQ), seq),
            seq_spec((KVW, SEQ), seq),
            seq_spec((KVW, SEQ), seq),
            seq_spec((HEADS, SEQ, SEQ), seq),
            seq_spec((D, SEQ), seq),
            seq_spec((D, SEQ), seq),
        ]
        + [pl.BlockSpec(memory_space=pl.ANY)] * len(after),
        out_specs=[whole_spec((QKV, SEQ)), whole_spec((8, 128))],
        out_shape=[
            jax.ShapeDtypeStruct((QKV, SEQ), BF16),
            jax.ShapeDtypeStruct((8, 128), F32),
        ],
        scratch_shapes=[
            pltpu.VMEM((D + KVW, SEQ), F32),
            pltpu.VMEM((KV_HEADS, SEQ, HEAD), BF16),
        ],
        compiler_params=pltpu.CompilerParams(vmem_limit_bytes=(63 if seq == 0 else 40) * 2**20),
        cost_estimate=pl.CostEstimate(flops=8 * 10**9, bytes_accessed=8 * 10**6, transcendentals=0),
        name="attn_bwd",
    )(*args, *after)


def qkv_bwd_kernel(
    where_ref, w_ref, gain_ref, dgain_two_ref, x_ref, h_t_ref, dx1_ref, dqkv0_ref, dqkv1_ref, *rest
):
    gx_ref, send_ref, keep_ref, zero_ref = rest[-11:-7]
    dw_ref, dgain_ref, qs_ref, ks_ref, vs_ref, gs_ref, stage_ref = rest[-7:]
    zero_ref[...] = jnp.zeros_like(zero_ref)
    dw = jnp.zeros((D, QKV), F32)
    dgain = jnp.zeros((D, 1), F32)
    for seq, dqkv_ref in enumerate((dqkv0_ref, dqkv1_ref)):
        dqkv = dqkv_ref[...]
        dh = mm(w_ref[...], dqkv)
        dw += mm(h_t_ref[seq], dqkv, NT)
        x = x_ref[seq].astype(F32)
        inv = lax.rsqrt(jnp.mean(x * x, axis=0, keepdims=True) + EPSILON)
        normed = x * inv
        dn = dh * gain_ref[:D]
        gx_ref[seq] = dx1_ref[seq] + inv * (
            dn - normed * jnp.mean(dn * normed, axis=0, keepdims=True)
        )
        dgain += jnp.sum(dh * normed, axis=1, keepdims=True)
    dw_ref[...] = dw
    dgain_ref[:D] = dgain
    dgain_ref[D:] = dgain_two_ref[...]
    join_square(qs_ref, dw_ref)
    for half in range(2):
        at = D + 96 * half
        ks_ref[pl.ds(half, D, stride=2), :96] = dw_ref[:, at : at + 96]
        vs_ref[pl.ds(half, D, stride=2), :96] = dw_ref[:, at + KVW : at + KVW + 96]
    for lane in range(9):
        gs_ref[:, lane : lane + 1] = dgain_ref[pl.ds(lane, 2 * CHIPS, stride=9), :]
    core = where_ref[0]
    stage_ref[...] = jnp.zeros_like(stage_ref)

    def spread(slot, carry):
        chip = chip_of(slot, where_ref, False)
        for keep_it in range(2):
            dev = chip * 2 + (core if keep_it else 1 - core)
            stage_ref[Q_QUERY : Q_QUERY + R_OUT, :] = get_rows(qs_ref, dev, R_OUT)
            stage_ref[Q_KEY : Q_KEY + R_KEY, :] = get_rows(ks_ref, dev, R_KEY)
            stage_ref[Q_VALUE : Q_VALUE + R_KEY, :] = get_rows(vs_ref, dev, R_KEY)
            stage_ref[Q_GAIN : Q_GAIN + 1, :] = get_rows(gs_ref, dev, 1)
            (keep_ref if keep_it else send_ref)[slot] = stage_ref[...].astype(BF16)
        return carry

    lax.fori_loop(0, CHIPS, spread, 0)


def qkv_bwd(args, after):
    seqs = args[4].shape[0]
    vmem = pl.BlockSpec(memory_space=pltpu.VMEM)
    return pl.pallas_call(
        qkv_bwd_kernel,
        in_specs=[pl.BlockSpec(memory_space=pltpu.SMEM)]
        + [vmem] * (len(args) - 1)
        + [pl.BlockSpec(memory_space=pl.ANY)] * len(after),
        out_specs=[vmem] * 4,
        out_shape=[
            jax.ShapeDtypeStruct((seqs, D, SEQ), F32),
            jax.ShapeDtypeStruct((CHIPS, ROWS_Q, 128), BF16),
            jax.ShapeDtypeStruct((CHIPS, ROWS_Q, 128), BF16),
            jax.ShapeDtypeStruct((8, 128), F32),
        ],
        scratch_shapes=[
            pltpu.VMEM((D, QKV), F32),
            pltpu.VMEM((2 * D, 1), F32),
            pltpu.VMEM((2 * CHIPS * R_OUT, 128), F32),
            pltpu.VMEM((2 * CHIPS * R_KEY, 128), F32),
            pltpu.VMEM((2 * CHIPS * R_KEY, 128), F32),
            pltpu.VMEM((2 * CHIPS, 128), F32),
            pltpu.VMEM((ROWS_Q, 128), F32),
        ],
        compiler_params=pltpu.CompilerParams(vmem_limit_bytes=40 * 2**20),
        cost_estimate=pl.CostEstimate(flops=8 * 10**9, bytes_accessed=12 * 10**6, transcendentals=0),
        name="qkv_bwd",
    )(*args, *after)


def pairs(axis, step):
    out = []
    for x in range(4):
        for y in range(4):
            for z in range(4):
                for core in range(2):
                    to = {"x": x, "y": y, "z": z, "c": core}
                    to[axis] = (to[axis] + step) % (2 if axis == "c" else 4)
                    me = ((x * 4 + y) * 4 + z) * 2 + core
                    out.append((me, ((to["x"] * 4 + to["y"]) * 4 + to["z"]) * 2 + to["c"]))
    return out


def hop(v, axis, step):
    return lax.ppermute(v, "dp", pairs(axis, step))


def sum_near(v, axis):
    low = v[1:].astype(BF16)
    got = [hop(low[k - 1], axis, k) for k in (2, 1, 3)]
    total = v[0].astype(F32)
    for piece in got:
        total = total + piece.astype(F32)
    return total


def both(keep, got, place, zero):
    rows = keep.shape[1]
    keep = keep.reshape(4, 4, 4, rows, 128)[place]
    got = got.reshape(4, 4, 4, rows, 128)[place]
    return keep.astype(F32) + got.astype(F32) + zero[0, 0]


def ring_far(far, axis):
    return hop(far[:2], axis, 1).astype(F32), hop(far[2:], axis, 3).astype(F32)


def ring_near(keep, got, arrived, zero):
    ahead, behind = both(keep, got, 1, zero), both(keep, got, 3, zero)
    ahead = jnp.concatenate([ahead[:2] + arrived[0], ahead[2:]])
    behind = jnp.concatenate([behind[:2], behind[2:] + arrived[1]])
    return ahead.astype(BF16), behind.astype(BF16)


def on_device(
    tokens, positions, norm_gains, w_query, w_key, w_value, w_out, w_gate, w_up, w_down, cotangent
):
    me = lax.axis_index("dp").astype(jnp.int32)
    where = jnp.stack([me % 2, me // 32, (me // 8) % 4, (me // 2) % 4])
    seqs = tokens.shape[0]
    x_t = jnp.swapaxes(tokens, 1, 2)
    cot_t = jnp.swapaxes(cotangent, 1, 2)

    pack_f = pack(
        [
            w_gate.reshape(R_GATE, 128),
            w_up.reshape(R_GATE, 128),
            lane_rows(w_down, 12, D),
            lane_rows(w_out, 9, 288),
        ],
        (F_GATE, F_UP, F_DOWN, F_OUT),
        ROWS_F,
        [],
    )
    pack_q = pack(
        [
            lane_rows(w_query, 9, 288),
            w_key.reshape(9, 96),
            w_value.reshape(9, 96),
            norm_gains.reshape(1, 9),
        ],
        (Q_QUERY, Q_KEY, Q_VALUE, Q_GAIN),
        ROWS_Q,
        [pack_f],
    )
    all_f = lax.all_gather(pack_f, "dp", axis=0, tiled=False)
    all_q = lax.all_to_all(
        jnp.broadcast_to(pack_q[None], (2 * CHIPS, ROWS_Q, 128)), "dp", split_axis=0, concat_axis=0
    )

    freqs = 100000.0 ** (-(jnp.arange(HEAD // 2, dtype=F32) * 2.0 / HEAD))
    angles = positions.astype(F32)[:, None, :] * freqs[None, :, None]
    cos_t = jnp.cos(angles)
    sin_t = jnp.sin(angles)
    fresh = (positions[:, 1:] != positions[:, :-1] + 1).astype(jnp.int32)
    docs = jnp.cumsum(jnp.pad(fresh, ((0, 0), (1, 0))), axis=1)

    wqkv, gain, h_t, q_t, k_t, v_t, p, o_t = attn_fwd(
        all_q, x_t, cos_t, sin_t, docs[:, None, :], docs[:, :, None]
    )
    y_t, dx1, do_t, dgain_two, send_g, keep_g, send_b, keep_b = ffn(
        where, all_f, x_t, o_t, cot_t, gain
    )
    got_g = hop(send_g, "c", 1)
    got_b = hop(send_b, "c", 1)
    args = [cos_t, sin_t, q_t, k_t, v_t, p, o_t, do_t]
    dqkv0, zero = attn_bwd(0, args, [])
    far_g = both(keep_g, got_g, 2, zero).astype(BF16)
    far_b = both(keep_b, got_b, 2, zero).astype(BF16)
    dqkv1, zero = attn_bwd(1, args, [far_g, far_b])
    near_g = ring_near(keep_g, got_g, ring_far(far_g, "z"), zero)
    near_b = ring_near(keep_b, got_b, ring_far(far_b, "y"), zero)
    gx_t, send_q, keep_q, zero = qkv_bwd(
        [where, wqkv, gain, dgain_two, x_t, h_t, dx1, dqkv0, dqkv1], near_g + near_b
    )
    got_q = hop(send_q, "c", 1)
    sum_g = both(keep_g, got_g, 0, zero)
    sum_g = sum_g + hop(near_g[0], "z", 1).astype(F32) + hop(near_g[1], "z", 3).astype(F32)
    sum_b = both(keep_b, got_b, 0, zero)
    sum_b = sum_b + hop(near_b[0], "y", 1).astype(F32) + hop(near_b[1], "y", 3).astype(F32)
    sum_q = (keep_q.astype(F32) + got_q.astype(F32)).reshape(4, 4, 4, ROWS_Q, 128)
    sum_q = sum_near(sum_q, "z")
    sum_b = sum_near(sum_b, "z")
    sum_a = sum_near(jnp.concatenate([sum_g, sum_q], axis=2), "y")
    final = sum_near(jnp.concatenate([sum_a, sum_b], axis=1), "x")
    fg = final[:ROWS_G]
    fq = final[ROWS_G : ROWS_G + ROWS_Q]
    fb = final[ROWS_G + ROWS_Q :]
    return (
        jnp.swapaxes(y_t, 1, 2),
        jnp.swapaxes(gx_t, 1, 2),
        take_lanes(fq[Q_GAIN : Q_GAIN + 1], 1, 9),
        take_lanes(fq[Q_QUERY : Q_QUERY + R_OUT], 9, 288),
        take_lanes(fq[Q_KEY : Q_KEY + R_KEY], 9, 96),
        take_lanes(fq[Q_VALUE : Q_VALUE + R_KEY], 9, 96),
        take_lanes(fg[G_OUT : G_OUT + R_OUT], 9, 288),
        fb[B_GATE : B_GATE + R_GATE].reshape(-1),
        fb[B_UP : B_UP + R_GATE].reshape(-1),
        take_lanes(fg[G_DOWN : G_DOWN + R_DOWN], 12, D),
    )


def solution(mesh):
    flat = P("dp")
    cube = P("dp", None, None)
    return jax.shard_map(
        on_device,
        mesh=mesh,
        in_specs=(cube, P("dp", None)) + (flat,) * 8 + (cube,),
        out_specs=(cube, cube) + (flat,) * 8,
        check_vma=False,
    )
```
